512 devices in a mesh: pix: 512 (over x, z, y, core).
Axes of the slice: x: 4, y: 8, z: 8, core: 2. Of those that a mesh axis runs over, the one named last changes fastest.
Arguments:
- input_maps: bfloat16 [64, 131072], P(None, 'pix'), may hold values from -6 to 6
- cheb_weights: bfloat16 [5, 64, 64], replicated, may hold values from -0.3125 to 0.3125
- cotangent: bfloat16 [64, 131072], P(None, 'pix'), may hold values from -6 to 6
- neighbours: int32 [9, 131072], P(None, 'pix'), may hold values from 0 to 767, as said below
- lap_weights: float32 [9, 131072], P(None, 'pix'), may hold values from -0.25 to 0.25
- send_rows: int32 [4096, 64], P('pix'), may hold values from 0 to 256, as said below
Outputs:
- output_maps: bfloat16 [64, 131072], P(None, 'pix')
- map_gradient: bfloat16 [64, 131072], P(None, 'pix')
- weight_gradient: float32 [5, 64, 64], replicated
The draws below stay inside these ranges and needn't reach their ends.
Inputs may be any that keep to these rules, and one draw needn't show every extreme that they name: `send_rows`: with offset_o = 1, -1, 16, -16, 17, 15, 1 - 16, -1 - 16: row 8 * d + o lists pixels of device d (numbered 0 to 255 within the device) that device (d + offset_o) mod 512 reads. Its live entries come first and are distinct; there are 32 to 64 of them, and for each o some device's list is full. The other entries equal 256. neighbours[0, p] is p's own column of extended_d. Every other entry is a column of the device's own pixels or a received column whose list entry is live. Each live received column 256 + o * 64 + j is read by exactly one pixel of the device, in entry 1 + o.
All inputs are finite; a program needn't handle non-finite values.
Results may differ from the reference program's by a relative error of at most 0.0046.
Values sent between devices are 32-bit elements; how exact they have to be, the bound alone decides.
A program may use at most 64 MiB of HBM per device.

```python
import math
import jax
import jax.numpy as jnp

CIN = 64
COUT = 64
KTERMS = 5
PIX_DEV = 256
HALO = 64
TILE_ROW = 16
PEERS = 8
STENCIL = 9
NPIX = 131072
N_PIX = 512


def peer_offsets_drawn():
    return [1, -1, TILE_ROW, -TILE_ROW, TILE_ROW + 1, TILE_ROW - 1, 1 - TILE_ROW, -1 - TILE_ROW]


def draw_plan(key):
    base_key = jax.random.fold_in(key, 4242)
    count_key, full_key, send_key, target_key, jitter_key = jax.random.split(base_key, 5)
    counts = jax.random.randint(count_key, (N_PIX, PEERS), HALO // 2, HALO + 1)
    full_device = jax.random.randint(full_key, (PEERS,), 0, N_PIX)
    device_ids = jnp.arange(N_PIX)
    counts = jnp.where(device_ids[:, None] == full_device[None, :], HALO, counts)
    send_keys = jax.random.split(send_key, N_PIX * PEERS)
    chosen = jax.vmap(lambda sub_key: jax.random.permutation(sub_key, PIX_DEV)[:HALO])(send_keys)
    chosen = chosen.reshape(N_PIX, PEERS, HALO)
    target_keys = jax.random.split(target_key, N_PIX * PEERS)
    targets = jax.vmap(lambda sub_key: jax.random.permutation(sub_key, PIX_DEV)[:HALO])(target_keys)
    targets = targets.reshape(N_PIX, PEERS, HALO)
    return (counts, chosen, targets, jitter_key)


def draw_send_rows(key, part):
    counts, chosen, targets, jitter_key = draw_plan(key)
    live_slots = jnp.arange(HALO)[None, None, :] < counts[:, :, None]
    listed = jnp.where(live_slots, chosen, PIX_DEV)
    return listed.reshape(N_PIX * PEERS, HALO).astype(jnp.int32)


def draw_neighbours(key, part):
    counts, chosen, targets, jitter_key = draw_plan(key)
    pixel_ids = jnp.arange(PIX_DEV)
    jitter = jax.random.randint(jitter_key, (STENCIL, N_PIX, PIX_DEV), -32, 33)
    local_rows = jnp.clip(pixel_ids[None, None, :] + jitter, 0, PIX_DEV - 1)
    device_ids = jnp.arange(N_PIX)
    offsets = jnp.array(peer_offsets_drawn())
    sources = (device_ids[:, None] - offsets[None, :]) % N_PIX
    peer_ids = jnp.arange(PEERS)
    incoming = counts[sources, peer_ids[None, :]]
    slot_ids = jnp.arange(HALO)
    columns = PIX_DEV + peer_ids[None, :, None] * HALO + slot_ids[None, None, :]
    live_slots = slot_ids[None, None, :] < incoming[:, :, None]
    columns = jnp.where(live_slots, columns, -1)
    halo_map = jnp.full((N_PIX, PEERS, PIX_DEV), -1, jnp.int32)
    halo_map = halo_map.at[device_ids[:, None, None], peer_ids[None, :, None], targets].set(columns.astype(jnp.int32))
    halo_map = jnp.transpose(halo_map, (1, 0, 2))
    others = jnp.where(halo_map >= 0, halo_map, local_rows[1:])
    own_rows = jnp.broadcast_to(pixel_ids[None, None, :], (1, N_PIX, PIX_DEV))
    entries = jnp.concatenate([own_rows, others], axis=0)
    return entries.reshape(STENCIL, NPIX).astype(jnp.int32)


def block_levels(rng, shape, shards, smallest, largest):
    gain = 1.0
    for axis_at, shards_of in shards:
        steps = jax.random.uniform(jax.random.fold_in(jax.random.fold_in(rng, 6), axis_at), (shards_of,), jnp.float32, smallest / len(shards), largest / len(shards))
        gain = gain * jnp.repeat(jnp.exp(steps), shape[axis_at] // shards_of).reshape((-1,) + (1,) * (len(shape) - 1 - axis_at))
    return gain


def scatter_about(rng, shape, scale, bound, shards=(), kind=jnp.bfloat16):
    gain = block_levels(rng, shape, shards, -0.22, 0.18) if shards else 1.0
    result = jax.random.normal(rng, shape, jnp.float32) * scale * gain
    return jnp.minimum(jnp.maximum(result, -bound), bound).astype(kind)


def setup_inputs(seed: int = 0) -> dict:
    streams_of = jax.random.split(jax.random.key(seed), 7)
    input_maps = scatter_about(streams_of[0], (CIN, NPIX), 1.0, 6.0, ((1, 512),))
    cheb_weights = scatter_about(streams_of[1], (KTERMS, CIN, COUT), (KTERMS * CIN) ** -0.5, 0.3125)
    cotangent = scatter_about(streams_of[2], (COUT, NPIX), 1.0, 6.0, ((1, 512),))
    neighbours = draw_neighbours(jax.random.fold_in(streams_of[6], 71), 0)
    lap_weights = jnp.clip(jax.random.uniform(streams_of[4], (STENCIL, NPIX), jnp.float32, -0.25, 0.25) * block_levels(streams_of[4], (STENCIL, NPIX), ((1, 512),), -0.4, 0.0), -0.25, 0.25)
    send_rows = draw_send_rows(jax.random.fold_in(streams_of[6], 71), 0)
    return {"input_maps": input_maps, "cheb_weights": cheb_weights, "cotangent": cotangent, "neighbours": neighbours, "lap_weights": lap_weights, "send_rows": send_rows}


def peer_offsets():
    return [1, -1, TILE_ROW, -TILE_ROW, TILE_ROW + 1, TILE_ROW - 1, 1 - TILE_ROW, -1 - TILE_ROW]

def source_devices(offset):
    devices = jnp.arange(N_PIX, dtype=jnp.int32)
    return (devices - offset) % N_PIX

def apply_forward(values, neighbours3, weights3, sends3):
    ext_width = PIX_DEV + PEERS * HALO
    padded = jnp.concatenate([values, jnp.zeros((CIN, N_PIX, 1), jnp.float32)], axis=2)
    padded = padded.reshape(CIN, N_PIX * (PIX_DEV + 1))
    blocks = [values]
    for peer_index, offset in enumerate(peer_offsets()):
        sources = source_devices(offset)
        columns = sources[:, None] * (PIX_DEV + 1) + sends3[sources, peer_index]
        blocks.append(padded[:, columns])
    extended = jnp.concatenate(blocks, axis=2).reshape(CIN, N_PIX * ext_width)
    devices = jnp.arange(N_PIX, dtype=jnp.int32)
    summed = jnp.zeros((CIN, N_PIX, PIX_DEV), jnp.float32)
    for stencil_slot in range(STENCIL):
        columns = devices[:, None] * ext_width + neighbours3[stencil_slot]
        summed = summed + weights3[stencil_slot][None] * extended[:, columns]
    return summed

def apply_adjoint(values, neighbours3, weights3, sends3):
    ext_width = PIX_DEV + PEERS * HALO
    devices = jnp.arange(N_PIX, dtype=jnp.int32)
    spread = jnp.zeros((CIN, N_PIX * ext_width), jnp.float32)
    for stencil_slot in range(STENCIL):
        columns = devices[:, None] * ext_width + neighbours3[stencil_slot]
        spread = spread.at[:, columns].add(weights3[stencil_slot][None] * values)
    spread = spread.reshape(CIN, N_PIX, ext_width)
    returned = jnp.zeros((CIN, N_PIX * (PIX_DEV + 1)), jnp.float32)
    for peer_index, offset in enumerate(peer_offsets()):
        sources = source_devices(offset)
        columns = sources[:, None] * (PIX_DEV + 1) + sends3[sources, peer_index]
        lower = PIX_DEV + peer_index * HALO
        returned = returned.at[:, columns].add(spread[:, :, lower:lower + HALO])
    returned = returned.reshape(CIN, N_PIX, PIX_DEV + 1)
    return spread[:, :, :PIX_DEV] + returned[:, :, :PIX_DEV]

def reference(input_maps, cheb_weights, cotangent, neighbours, lap_weights, send_rows):
    neighbours3 = neighbours.reshape(STENCIL, N_PIX, PIX_DEV)
    weights3 = lap_weights.reshape(STENCIL, N_PIX, PIX_DEV)
    sends3 = send_rows.reshape(N_PIX, PEERS, HALO)
    zeroth = input_maps.astype(jnp.float32).reshape(CIN, N_PIX, PIX_DEV)
    terms = [zeroth, apply_forward(zeroth, neighbours3, weights3, sends3)]
    for term_index in range(2, KTERMS):
        terms.append(2.0 * apply_forward(terms[-1], neighbours3, weights3, sends3) - terms[-2])
    stacked = jnp.concatenate([one_term.astype(jnp.bfloat16).reshape(CIN, NPIX) for one_term in terms], axis=0)
    flat_weights = cheb_weights.reshape(KTERMS * CIN, COUT)
    output_maps = jnp.dot(flat_weights.T, stacked, preferred_element_type=jnp.float32).astype(jnp.bfloat16)
    weight_gradient = jnp.dot(stacked, cotangent.T, preferred_element_type=jnp.float32) / math.sqrt(NPIX)
    weight_gradient = weight_gradient.reshape(KTERMS, CIN, COUT)
    adjoints = jnp.dot(flat_weights, cotangent, preferred_element_type=jnp.float32)
    adjoints = adjoints.reshape(KTERMS, CIN, N_PIX, PIX_DEV)
    adjoint_list = [adjoints[term_index] for term_index in range(KTERMS)]
    for term_index in range(KTERMS - 1, 1, -1):
        carried = apply_adjoint(adjoint_list[term_index], neighbours3, weights3, sends3)
        adjoint_list[term_index - 1] = adjoint_list[term_index - 1] + 2.0 * carried
        adjoint_list[term_index - 2] = adjoint_list[term_index - 2] - adjoint_list[term_index]
    adjoint_list[0] = adjoint_list[0] + apply_adjoint(adjoint_list[1], neighbours3, weights3, sends3)
    map_gradient = adjoint_list[0].reshape(CIN, NPIX).astype(jnp.bfloat16)
    return (output_maps, map_gradient, weight_gradient)
```

```python
import math

import jax
import jax.numpy as jnp
from jax import lax
from jax.experimental import pallas as pl
from jax.experimental.pallas import tpu as pltpu
from jax.sharding import PartitionSpec as P

CH = 64
KTERMS = 5
PIX = 256
HALO = 64
ROW = 16
PEERS = 8
STENCIL = 9
STEPS = KTERMS - 1
OFFSETS = [1, -1, 16, -16, 17, 15, -15, -17]
ORDER = [0, 1, 2, 3, 4, 7, 5, 6]
PART = 10
MESH = pl.DeviceIdType.MESH
F32 = jnp.float32
BF16 = jnp.bfloat16


def split(value):
    high = value.astype(BF16)
    return high, (value - high.astype(F32)).astype(BF16)


def dot(a, b):
    return jnp.dot(a, b, preferred_element_type=F32)


def dot_nt(a, b):
    return lax.dot_general(a, b, (((1,), (1,)), ((), ())), preferred_element_type=F32)


def product(value, high, low, times):
    value_high, value_low = split(value)
    both = times(jnp.concatenate([value_high, value_low], axis=0), high)
    result = both[:CH] + both[CH:]
    if low is not None:
        result = result + times(value_high, low)
    return result


def kernel(
    count,
    x_ref,
    w_ref,
    ct_ref,
    nb_ref,
    lw_ref,
    sends_ref,
    out_ref,
    mg_ref,
    wg_ref,
    a_high,
    a_low,
    h_high,
    h_low,
    s_mat,
    outgoing,
    incoming,
    sums,
    row_in,
    part,
    column_in,
    total,
    halo_send,
    halo_recv,
    row_send,
    row_recv,
    column_send,
    column_recv,
    last_send,
    last_recv,
):
    me = lax.axis_index("pix")
    rows = count // ROW
    my_row, my_column = me // ROW, me % ROW
    peers = [(me + OFFSETS[o] + count) % count for o in ORDER]

    def row_peer(step):
        return (my_column + step) % ROW

    def column_peer(step):
        return (my_row + step) % rows

    barrier = pltpu.get_barrier_semaphore()
    for peer in peers:
        pl.semaphore_signal(barrier, inc=1, device_id=(peer,), device_id_type=MESH)

    @pl.loop(1, ROW)
    def _(step):
        target = my_row * ROW + row_peer(step)
        pl.semaphore_signal(barrier, inc=1, device_id=(target,), device_id_type=MESH)

    @pl.loop(1, rows)
    def _(step):
        target = column_peer(step) * ROW + my_column
        pl.semaphore_signal(barrier, inc=1, device_id=(target,), device_id_type=MESH)

    lane_low = lax.broadcasted_iota(jnp.int32, (CH, 128), 1) < HALO

    for pair in range(PEERS // 2):
        listed = jnp.concatenate(
            [sends_ref[ORDER[2 * pair + i] : ORDER[2 * pair + i] + 1, :] for i in range(2)], axis=1
        )
        pixel = lax.broadcasted_iota(jnp.int32, (PIX, 128), 0)
        s_mat[:, 128 * pair : 128 * pair + 128] = jnp.where(pixel == listed, 1.0, 0.0).astype(BF16)
    for place, o in enumerate(ORDER):
        slot = lax.broadcasted_iota(jnp.int32, (HALO, PIX), 0) + (PIX + HALO * o)
        block = jnp.where(slot == nb_ref[o + 1 : o + 2, :], lw_ref[o + 1 : o + 2, :], 0.0)
        high, low = split(block)
        h_high[HALO * place : HALO * place + HALO, :] = high
        h_low[HALO * place : HALO * place + HALO, :] = low
    for base in range(0, PIX, 32):
        column = lax.broadcasted_iota(jnp.int32, (32, PIX), 0) + base
        block = jnp.zeros((32, PIX), F32)
        for slot in range(STENCIL):
            block = block + jnp.where(
                column == nb_ref[slot : slot + 1, :], lw_ref[slot : slot + 1, :], 0.0
            )
        high, low = split(block)
        a_high[base : base + 32, :] = high
        a_low[base : base + 32, :] = low

    weights = [w_ref[CH * k : CH * k + CH, :] for k in range(KTERMS)]

    def out_term(k, term):
        turned = lax.dot_general(
            weights[k],
            term.astype(BF16),
            (((0,), (0,)), ((), ())),
            preferred_element_type=F32,
        )
        return turned

    def mg_term(k, term):
        high, low = split(term)
        return dot(weights[k], high) + dot(weights[k], low)

    def halo_copy(step, place):
        return pltpu.make_async_remote_copy(
            src_ref=outgoing.at[step, place],
            dst_ref=incoming.at[step, place],
            send_sem=halo_send.at[step, place],
            recv_sem=halo_recv.at[step, place],
            device_id=(peers[place],),
            device_id_type=MESH,
        )

    def row_copy(step):
        other = row_peer(step)
        return pltpu.make_async_remote_copy(
            src_ref=sums.at[other],
            dst_ref=row_in.at[my_column],
            send_sem=row_send.at[other],
            recv_sem=row_recv.at[my_column],
            device_id=(my_row * ROW + other,),
            device_id_type=MESH,
        )

    def row_arrival(step):
        other = row_peer(step)
        return pltpu.make_async_remote_copy(
            src_ref=sums.at[other],
            dst_ref=row_in.at[other],
            send_sem=row_send.at[other],
            recv_sem=row_recv.at[other],
            device_id=(my_row * ROW + other,),
            device_id_type=MESH,
        )

    def column_copy(step, arrival):
        other = column_peer(step)
        place = other if arrival else my_row
        return pltpu.make_async_remote_copy(
            src_ref=part,
            dst_ref=column_in.at[place],
            send_sem=column_send.at[other],
            recv_sem=column_recv.at[place],
            device_id=(other * ROW + my_column,),
            device_id_type=MESH,
        )

    def last_copy(step, arrival):
        other = row_peer(step)
        place = other if arrival else my_column
        return pltpu.make_async_remote_copy(
            src_ref=total.at[my_column],
            dst_ref=total.at[place],
            send_sem=last_send.at[other],
            recv_sem=last_recv.at[place],
            device_id=(my_row * ROW + other,),
            device_id_type=MESH,
        )

    xs = [x_ref[...].astype(F32)]
    cs = [ct_ref[...].astype(F32)]
    out_sum = out_term(0, xs[0])
    mg_sum = mg_term(0, cs[0])
    pl.semaphore_wait(barrier, PEERS + ROW - 1 + rows - 1)

    for step in range(STEPS):
        x, c = xs[-1], cs[-1]
        gathered = product(x, s_mat[...], None, dot)
        returned = product(c, h_high[...], h_low[...], dot_nt)
        for pair in range(PEERS // 2):
            forward = gathered[:, 128 * pair : 128 * pair + 128]
            back = returned[:, 128 * pair : 128 * pair + 128]
            outgoing[step, 2 * pair] = jnp.where(lane_low, forward, back)
            halo_copy(step, 2 * pair).start()
            outgoing[step, 2 * pair + 1] = jnp.where(lane_low, back, forward)
            halo_copy(step, 2 * pair + 1).start()
        if step == 2:
            scale = 1.0 / math.sqrt(count * PIX)
            c0 = cs[0].astype(BF16)
            early = dot_nt(jnp.concatenate([t.astype(BF16) for t in xs], axis=0), c0)
            c_high, c_low = split(jnp.concatenate([cs[1], cs[2]], axis=0))
            x_high, x_low = split(xs[2])
            late = dot_nt(x_high, c_high) + dot_nt(x_low, c_high) + dot_nt(x_high, c_low)
            p0, p1, p2 = early[:CH], early[CH : 2 * CH], early[2 * CH :]
            first = jnp.concatenate([p1, p2], axis=1) * scale
            second = (2.0 * late - jnp.concatenate([p1, p0], axis=1)) * scale
            third = jnp.concatenate([p0[:32], p0[32:]], axis=1) * scale
            for i in range(ROW):
                sums[i, 0:4, :] = first[4 * i : 4 * i + 4]
                sums[i, 4:8, :] = second[4 * i : 4 * i + 4]
                sums[i, 8:10, :] = third[2 * i : 2 * i + 2]

            @pl.loop(1, ROW)
            def _(i):
                row_copy(i).start()

            row_in[my_column] = sums[my_column]
        if step == 3:

            @pl.loop(1, ROW)
            def _(i):
                row_arrival(i).wait_recv()

            piece = row_in[0]
            for i in range(1, ROW):
                piece = piece + row_in[i]
            part[...] = piece
            column_in[my_row] = piece

            @pl.loop(1, rows)
            def _(i):
                column_copy(i, False).start()

        x_near = product(x, a_high[...], a_low[...], dot)
        c_near = product(c, a_high[...], a_low[...], dot_nt)
        if step:
            out_sum = out_sum + out_term(step, x)
            mg_sum = mg_sum + mg_term(step, c)
        x_far, c_far = [], []
        for pair in range(PEERS // 2):
            halo_copy(step, 2 * pair).wait_recv()
            halo_copy(step, 2 * pair + 1).wait_recv()
            one, two = incoming[step, 2 * pair], incoming[step, 2 * pair + 1]
            x_far.append(jnp.where(lane_low, one, two))
            c_far.append(jnp.where(lane_low, two, one))
        x_sum = x_near + product(jnp.concatenate(x_far, axis=1), h_high[...], h_low[...], dot)
        c_sum = c_near + product(jnp.concatenate(c_far, axis=1), s_mat[...], None, dot_nt)
        if step:
            x_sum = 2.0 * x_sum - xs[-2]
            c_sum = 2.0 * c_sum - cs[-2]
        xs.append(x_sum)
        cs.append(c_sum)

    @pl.loop(1, rows)
    def _(i):
        column_copy(i, True).wait_recv()

    piece = column_in[0]
    for i in range(1, rows):
        piece = piece + column_in[i]
    total[my_column] = piece

    @pl.loop(1, ROW)
    def _(i):
        last_copy(i, False).start()

    out_ref[...] = (out_sum + out_term(STEPS, xs[-1])).astype(BF16)
    mg_ref[...] = (mg_sum + mg_term(STEPS, cs[-1])).astype(BF16)

    @pl.loop(1, ROW)
    def _(i):
        last_copy(i, True).wait_recv()

    def half(pieces, side):
        return jnp.concatenate(pieces, axis=0)[:, CH * side : CH * side + CH]

    first = [total[i, 0:4, :] for i in range(ROW)]
    second = [total[i, 4:8, :] for i in range(ROW)]
    third = [total[i, 8:10, :] for i in range(ROW)]
    wg_ref[0, 0:32] = half(third, 0)
    wg_ref[0, 32:64] = half(third, 1)
    wg_ref[1] = half(first, 0)
    wg_ref[2] = half(first, 1)
    wg_ref[3] = half(second, 0)
    wg_ref[4] = half(second, 1)

    for step in range(STEPS):
        for place in range(PEERS):
            halo_copy(step, place).wait_send()

    @pl.loop(1, ROW)
    def _(i):
        row_copy(i).wait_send()
        last_copy(i, False).wait_send()

    @pl.loop(1, rows)
    def _(i):
        column_copy(i, False).wait_send()


def solution(mesh):
    count = mesh.shape["pix"]
    rows = count // ROW
    dma = pltpu.SemaphoreType.DMA

    def local(input_maps, cheb_weights, cotangent, neighbours, lap_weights, send_rows):
        def body(*refs):
            kernel(count, *refs)

        return pl.pallas_call(
            body,
            out_shape=(
                jax.ShapeDtypeStruct((CH, PIX), BF16),
                jax.ShapeDtypeStruct((CH, PIX), BF16),
                jax.ShapeDtypeStruct((KTERMS, CH, CH), F32),
            ),
            in_specs=[pl.BlockSpec(memory_space=pltpu.VMEM)] * 6,
            out_specs=tuple([pl.BlockSpec(memory_space=pltpu.VMEM)] * 3),
            scratch_shapes=[
                pltpu.VMEM((PIX, PIX), BF16),
                pltpu.VMEM((PIX, PIX), BF16),
                pltpu.VMEM((PEERS * HALO, PIX), BF16),
                pltpu.VMEM((PEERS * HALO, PIX), BF16),
                pltpu.VMEM((PIX, PEERS * HALO), BF16),
                pltpu.VMEM((STEPS, PEERS, CH, 128), F32),
                pltpu.VMEM((STEPS, PEERS, CH, 128), F32),
                pltpu.VMEM((ROW, PART, 128), F32),
                pltpu.VMEM((ROW, PART, 128), F32),
                pltpu.VMEM((PART, 128), F32),
                pltpu.VMEM((rows, PART, 128), F32),
                pltpu.VMEM((ROW, PART, 128), F32),
                dma((STEPS, PEERS)),
                dma((STEPS, PEERS)),
                dma((ROW,)),
                dma((ROW,)),
                dma((rows,)),
                dma((rows,)),
                dma((ROW,)),
                dma((ROW,)),
            ],
            compiler_params=pltpu.CompilerParams(
                collective_id=0, has_side_effects=True, vmem_limit_bytes=32 * 1024 * 1024
            ),
        )(
            input_maps,
            cheb_weights.reshape(KTERMS * CH, CH),
            cotangent,
            neighbours,
            lap_weights,
            send_rows,
        )

    return jax.shard_map(
        local,
        mesh=mesh,
        in_specs=(
            P(None, "pix"),
            P(),
            P(None, "pix"),
            P(None, "pix"),
            P(None, "pix"),
            P("pix", None),
        ),
        out_specs=(P(None, "pix"), P(None, "pix"), P()),
        check_vma=False,
    )
```

```python
import math

import jax
import jax.numpy as jnp
from jax import lax
from jax.experimental import pallas as pl
from jax.experimental.pallas import tpu as pltpu
from jax.sharding import PartitionSpec as P

CH = 64
KTERMS = 5
PIX = 256
HALO = 64
ROW = 16
PEERS = 8
STENCIL = 9
STEPS = KTERMS - 1
OFFSETS = [1, -1, 16, -16, 17, 15, -15, -17]
ORDER = [0, 1, 2, 3, 4, 7, 5, 6]
LISTED = PEERS * HALO
SHARES = [6, 4]
MESH = pl.DeviceIdType.MESH
F32 = jnp.float32
BF16 = jnp.bfloat16


def split(value):
    high = value.astype(BF16)
    return high, (value - high.astype(F32)).astype(BF16)


def dot(a, b):
    return jnp.dot(a, b, preferred_element_type=F32)


def dot_nt(a, b):
    return lax.dot_general(a, b, (((1,), (1,)), ((), ())), preferred_element_type=F32)


def dot_tn(a, b):
    return lax.dot_general(a, b, (((0,), (0,)), ((), ())), preferred_element_type=F32)


def product(value, matrix, times):
    high, low = split(value)
    both = times(jnp.concatenate([high, low], axis=0), matrix)
    rows = value.shape[0]
    return both[:rows] + both[rows:]


def turned(value):
    return pltpu.roll(value, HALO, 1)


def kernel(
    count,
    x_hbm,
    w_hbm,
    ct_hbm,
    nb_hbm,
    lw_hbm,
    sends_hbm,
    out_ref,
    mg_ref,
    wg_ref,
    x_ref,
    w_ref,
    ct_ref,
    nb_ref,
    lw_ref,
    sends_ref,
    load_sem,
    a_high,
    a_low,
    s_mat,
    t_mat,
    outgoing,
    incoming,
    halo_send,
    halo_recv,
    sum_send,
    sum_recv,
    *sum_refs,
):
    me = lax.axis_index("pix")
    rows = count // ROW
    my_row, my_column = me // ROW, me % ROW
    peers = [(me + OFFSETS[o] + count) % count for o in ORDER]

    def in_row(step):
        return my_row * ROW + (my_column + step) % ROW

    def in_column(step):
        return (my_row + step) % rows * ROW + my_column

    barrier = pltpu.get_barrier_semaphore()

    def greet(device):
        pl.semaphore_signal(barrier, inc=1, device_id=(device,), device_id_type=MESH)

    for peer in peers:
        greet(peer)
    greet(in_row(1))
    greet(in_row(ROW - 1))

    loads = [
        pltpu.make_async_copy(src, dst, load_sem.at[i])
        for i, (src, dst) in enumerate(
            (
                (sends_hbm, sends_ref),
                (x_hbm, x_ref),
                (nb_hbm, nb_ref),
                (lw_hbm, lw_ref),
                (ct_hbm, ct_ref),
                (w_hbm, w_ref),
            )
        )
    ]
    for load in loads:
        load.start()

    @pl.loop(2, rows - 1)
    def _(step):
        greet(in_column(step))

    @pl.loop(2, ROW - 1)
    def _(step):
        greet(in_row(step))

    lane_low = lax.broadcasted_iota(jnp.int32, (CH // 2, 128), 1) < HALO

    def halo_copy(chain, step, place):
        return pltpu.make_async_remote_copy(
            src_ref=outgoing.at[chain, step, place],
            dst_ref=incoming.at[chain, step, place],
            send_sem=halo_send.at[chain, step],
            recv_sem=halo_recv.at[chain, step],
            device_id=(peers[place if chain == 0 else place ^ 1],),
            device_id_type=MESH,
        )

    def halo_all(chain, step):
        return pltpu.make_async_remote_copy(
            src_ref=outgoing.at[chain, step],
            dst_ref=incoming.at[chain, step],
            send_sem=halo_send.at[chain, step],
            recv_sem=halo_recv.at[chain, step],
            device_id=(peers[0],),
            device_id_type=MESH,
        )

    def post(chain, step, columns, start=True):
        for pair in range(PEERS // 2):
            block = columns[:, 128 * pair : 128 * pair + 128]
            upper, lower = block[: CH // 2], block[CH // 2 :]
            outgoing[chain, step, 2 * pair] = jnp.where(lane_low, upper, turned(lower))
            outgoing[chain, step, 2 * pair + 1] = jnp.where(lane_low, turned(upper), lower)
            if start:
                halo_copy(chain, step, 2 * pair).start()
                halo_copy(chain, step, 2 * pair + 1).start()

    def collect(chain, step):
        halo_all(chain, step).wait_recv()
        blocks = []
        for pair in range(PEERS // 2):
            one, two = incoming[chain, step, 2 * pair], incoming[chain, step, 2 * pair + 1]
            blocks.append(
                jnp.concatenate(
                    [jnp.where(lane_low, one, turned(two)), jnp.where(lane_low, turned(one), two)],
                    axis=0,
                )
            )
        return jnp.concatenate(blocks, axis=1)

    loads[0].wait()
    pixel = lax.broadcasted_iota(jnp.int32, (PIX, 128), 0)
    for pair in range(PEERS // 2):
        listed = jnp.concatenate(
            [sends_ref[ORDER[2 * pair + i] : ORDER[2 * pair + i] + 1, :] for i in range(2)], axis=1
        )
        s_mat[:, 128 * pair : 128 * pair + 128] = jnp.where(pixel == listed, 1.0, 0.0).astype(BF16)
    loads[1].wait()
    xs = [x_ref[...].astype(F32)]
    post(0, 0, dot(x_ref[...], s_mat[...]), start=False)
    loads[2].wait()
    slot = lax.broadcasted_iota(jnp.int32, (HALO, PIX), 0) + PIX
    for place, o in enumerate(ORDER):
        hit = slot + HALO * o == nb_ref[o + 1 : o + 2, :]
        t_mat[HALO * place : HALO * place + HALO, :] = jnp.where(hit, 1.0, 0.0).astype(BF16)
    loads[3].wait()
    lists = jnp.concatenate([lw_ref[o + 1 : o + 2, :] for o in ORDER], axis=0)
    high, rest = split(lists)
    middle = (lists - high.astype(F32)).astype(BF16)
    low = (lists - high.astype(F32) - middle.astype(F32)).astype(BF16)
    found = dot_nt(jnp.concatenate([high, middle, low], axis=0), t_mat[...])
    found = found[:PEERS] + found[PEERS : 2 * PEERS] + found[2 * PEERS :]
    own = lax.broadcasted_iota(jnp.int32, (PEERS, LISTED), 1) // HALO
    own = own == lax.broadcasted_iota(jnp.int32, (PEERS, LISTED), 0)
    list_weight = jnp.sum(jnp.where(own, found, 0.0), axis=0, keepdims=True)
    loads[4].wait()
    cs = [ct_ref[...].astype(F32)]
    post(1, 0, dot_nt(ct_ref[...], t_mat[...]) * list_weight, start=False)
    pl.semaphore_wait(barrier, PEERS + ROW - 1 + rows - 3)
    for chain in range(2):
        for place in range(PEERS):
            halo_copy(chain, 0, place).start()

    for base in range(0, PIX, 32):
        column = lax.broadcasted_iota(jnp.int32, (32, PIX), 0) + base
        block = jnp.zeros((32, PIX), F32)
        for entry in range(STENCIL):
            block = block + jnp.where(
                column == nb_ref[entry : entry + 1, :], lw_ref[entry : entry + 1, :], 0.0
            )
        high, low = split(block)
        a_high[base : base + 32, :] = high
        a_low[base : base + 32, :] = low
    loads[5].wait()

    def near(value, times):
        return product(value, a_high[...], times) + times(value.astype(BF16), a_low[...])

    def out_term(k):
        return dot_tn(w_ref[CH * k : CH * k + CH, :], xs[k].astype(BF16))

    def mg_term(k):
        high, low = split(cs[k])
        weight = w_ref[CH * k : CH * k + CH, :]
        return dot(weight, high) + dot(weight, low)

    def inner(x, c):
        x_high, x_low = split(x)
        c_high, c_low = split(c)
        both = dot_nt(jnp.concatenate([x_high, x_low], axis=0), c_high)
        return both[:CH] + both[CH:] + dot_nt(x_high, c_low)

    class Batch:
        def __init__(self, which):
            self.which = which
            self.sums, self.row_in, self.part, self.column_in, self.total = sum_refs[
                5 * which : 5 * which + 5
            ]

        def copy(self, stage, src, dst, device):
            return pltpu.make_async_remote_copy(
                src_ref=src,
                dst_ref=dst,
                send_sem=sum_send.at[self.which, stage],
                recv_sem=sum_recv.at[self.which, stage],
                device_id=(device,),
                device_id_type=MESH,
            )

        def all_of(self, stage):
            ref = (self.row_in, self.column_in, self.total)[stage]
            ref = ref.at[pl.ds(0, (ROW, rows, ROW)[stage] - 1)]
            return self.copy(stage, ref, ref, peers[0])

        def start(self, blocks):
            at = 0
            for block in blocks:
                n = block.shape[0] // ROW
                for i in range(ROW):
                    self.sums[i, at : at + n, :] = block[n * i : n * i + n]
                at += n

            @pl.loop(1, ROW)
            def _(i):
                other = (my_column + i) % ROW
                self.copy(
                    0, self.sums.at[other], self.row_in.at[my_column], my_row * ROW + other
                ).start()

            self.row_in[my_column] = self.sums[my_column]

        def across(self):
            self.all_of(0).wait_recv()
            piece = self.row_in[0]
            for i in range(1, ROW):
                piece = piece + self.row_in[i]
            self.part[...] = piece

            @pl.loop(1, rows)
            def _(i):
                self.copy(1, self.part, self.column_in.at[my_row], in_column(i)).start()

            self.column_in[my_row] = piece

        def back(self):
            self.all_of(1).wait_recv()
            piece = self.column_in[0]
            for i in range(1, rows):
                piece = piece + self.column_in[i]
            self.total[my_column] = piece

            @pl.loop(1, ROW)
            def _(i):
                mine = self.total.at[my_column]
                self.copy(2, mine, mine, in_row(i)).start()

        def arrive(self):
            self.all_of(2).wait_recv()

        def end(self):
            for stage in range(3):
                self.all_of(stage).wait_send()

    early, late = Batch(0), Batch(1)
    scale = 1.0 / math.sqrt(count * PIX)

    def halves(value):
        return jnp.concatenate([value[: CH // 2], value[CH // 2 :]], axis=1)

    out_sum = mg_sum = None
    for step in range(STEPS):
        x_near = near(xs[step], dot)
        c_near = near(cs[step], dot_nt)
        x_next = x_near + product(collect(0, step) * list_weight, t_mat[...], dot)
        if step:
            x_next = 2.0 * x_next - xs[step - 1]
        xs.append(x_next)
        if step + 1 < STEPS:
            post(0, step + 1, product(x_next, s_mat[...], dot))
        c_next = c_near + product(collect(1, step), s_mat[...], dot_nt)
        if step:
            c_next = 2.0 * c_next - cs[step - 1]
        cs.append(c_next)
        if step + 1 < STEPS:
            post(1, step + 1, product(c_next, t_mat[...], dot_nt) * list_weight)
        if step == 0:
            p0 = dot_nt(x_ref[...], ct_ref[...]) * scale
            p1 = dot_nt(xs[1].astype(BF16), ct_ref[...]) * scale
            p2 = inner(xs[1], cs[1]) * (2.0 * scale) - p0
            early.start([jnp.concatenate([p0, p1], axis=1), halves(p2)])
        if step == 1:
            last = inner(xs[2], jnp.concatenate([cs[1], cs[2]], axis=0)) * (2.0 * scale)
            late.start([last - jnp.concatenate([p1, p0], axis=1)])
            early.across()
        if step == 2:
            late.across()
            early.back()
        term_out, term_mg = out_term(step), mg_term(step)
        out_sum = term_out if out_sum is None else out_sum + term_out
        mg_sum = term_mg if mg_sum is None else mg_sum + term_mg

    out_ref[...] = (out_sum + out_term(STEPS)).astype(BF16)
    mg_ref[...] = (mg_sum + mg_term(STEPS)).astype(BF16)
    late.back()
    early.arrive()

    def rows_of(batch, lower, upper):
        return jnp.concatenate([batch.total[i, lower:upper, :] for i in range(ROW)], axis=0)

    first = rows_of(early, 0, 4)
    third = rows_of(early, 4, 6)
    wg_ref[0] = first[:, :CH]
    wg_ref[1] = first[:, CH:]
    wg_ref[2, : CH // 2] = third[:, :CH]
    wg_ref[2, CH // 2 :] = third[:, CH:]
    for chain in range(2):
        for step in range(STEPS):
            halo_all(chain, step).wait_send()
    early.end()
    late.arrive()
    second = rows_of(late, 0, 4)
    wg_ref[3] = second[:, :CH]
    wg_ref[4] = second[:, CH:]
    late.end()


def store_results(out_ref, mg_ref, wg_ref, out_hbm, mg_hbm, wg_hbm, sem):
    copies = [
        pltpu.make_async_copy(src, dst, sem.at[i])
        for i, (src, dst) in enumerate(((wg_ref, wg_hbm), (out_ref, out_hbm), (mg_ref, mg_hbm)))
    ]
    for copy in copies:
        copy.start()
    for copy in copies:
        copy.wait()


def solution(mesh):
    count = mesh.shape["pix"]
    rows = count // ROW
    dma = pltpu.SemaphoreType.DMA

    def local(input_maps, cheb_weights, cotangent, neighbours, lap_weights, send_rows):
        def body(*refs):
            kernel(count, *refs)

        results = pl.pallas_call(
            body,
            out_shape=(
                jax.ShapeDtypeStruct((CH, PIX), BF16),
                jax.ShapeDtypeStruct((CH, PIX), BF16),
                jax.ShapeDtypeStruct((KTERMS, CH, CH), F32),
            ),
            in_specs=[pl.BlockSpec(memory_space=pltpu.HBM)] * 6,
            out_specs=tuple([pl.BlockSpec(memory_space=pltpu.VMEM)] * 3),
            scratch_shapes=[
                pltpu.VMEM((CH, PIX), BF16),
                pltpu.VMEM((KTERMS * CH, CH), BF16),
                pltpu.VMEM((CH, PIX), BF16),
                pltpu.VMEM((STENCIL, PIX), jnp.int32),
                pltpu.VMEM((STENCIL, PIX), F32),
                pltpu.VMEM((PEERS, HALO), jnp.int32),
                dma((6,)),
                pltpu.VMEM((PIX, PIX), BF16),
                pltpu.VMEM((PIX, PIX), BF16),
                pltpu.VMEM((PIX, LISTED), BF16),
                pltpu.VMEM((LISTED, PIX), BF16),
                pltpu.VMEM((2, STEPS, PEERS, CH // 2, 128), F32),
                pltpu.VMEM((2, STEPS, PEERS, CH // 2, 128), F32),
                dma((2, STEPS)),
                dma((2, STEPS)),
                dma((2, 3)),
                dma((2, 3)),
                *[
                    pltpu.VMEM(lead + (share, 128), F32)
                    for share in SHARES
                    for lead in ((ROW,), (ROW,), (), (rows,), (ROW,))
                ],
            ],
            compiler_params=pltpu.CompilerParams(
                collective_id=0, has_side_effects=True, vmem_limit_bytes=60 * 1024 * 1024
            ),
        )(
            input_maps,
            cheb_weights.reshape(KTERMS * CH, CH),
            cotangent,
            neighbours,
            lap_weights,
            send_rows,
        )
        return pl.pallas_call(
            store_results,
            out_shape=tuple(jax.ShapeDtypeStruct(r.shape, r.dtype) for r in results),
            in_specs=[pl.BlockSpec(memory_space=pltpu.VMEM)] * 3,
            out_specs=tuple([pl.BlockSpec(memory_space=pltpu.HBM)] * 3),
            scratch_shapes=[dma((3,))],
        )(*results)

    return jax.shard_map(
        local,
        mesh=mesh,
        in_specs=(
            P(None, "pix"),
            P(),
            P(None, "pix"),
            P(None, "pix"),
            P(None, "pix"),
            P("pix", None),
        ),
        out_specs=(P(None, "pix"), P(None, "pix"), P()),
        check_vma=False,
    )
```

```python
import math

import jax
import jax.numpy as jnp
from jax import lax
from jax.experimental import pallas as pl
from jax.experimental.pallas import tpu as pltpu
from jax.sharding import PartitionSpec as P

CH = 64
KTERMS = 5
PIX = 256
HALO = 64
ROW = 16
PEERS = 8
STENCIL = 9
STEPS = KTERMS - 1
OFFSETS = [1, -1, 16, -16, 17, 15, -15, -17]
ORDER = [0, 1, 2, 3, 4, 7, 5, 6]
LISTED = PEERS * HALO
SHARES = [6, 4]
MESH = pl.DeviceIdType.MESH
F32 = jnp.float32
BF16 = jnp.bfloat16


def split(value):
    high = value.astype(BF16)
    return high, (value - high.astype(F32)).astype(BF16)


def dot(a, b):
    return jnp.dot(a, b, preferred_element_type=F32)


def dot_nt(a, b):
    return lax.dot_general(a, b, (((1,), (1,)), ((), ())), preferred_element_type=F32)


def dot_tn(a, b):
    return lax.dot_general(a, b, (((0,), (0,)), ((), ())), preferred_element_type=F32)


def product(value, matrix, times):
    high, low = split(value)
    both = times(jnp.concatenate([high, low], axis=0), matrix)
    rows = value.shape[0]
    return both[:rows] + both[rows:]


def turned(value):
    return pltpu.roll(value, HALO, 1)


def kernel(
    count,
    x_hbm,
    w_hbm,
    ct_hbm,
    nb_hbm,
    lw_hbm,
    sends_hbm,
    out_ref,
    mg_ref,
    wg_ref,
    x_ref,
    w_ref,
    ct_ref,
    nb_ref,
    lw_ref,
    sends_ref,
    load_sem,
    a_high,
    a_low,
    s_mat,
    t_mat,
    outgoing,
    incoming,
    halo_send,
    halo_recv,
    sum_send,
    sum_recv,
    *sum_refs,
):
    me = lax.axis_index("pix")
    rows = count // ROW
    my_row, my_column = me // ROW, me % ROW
    peers = [(me + OFFSETS[o] + count) % count for o in ORDER]

    def in_row(step):
        return my_row * ROW + (my_column + step) % ROW

    def in_column(step):
        return (my_row + step) % rows * ROW + my_column

    barrier = pltpu.get_barrier_semaphore()

    def greet(device):
        pl.semaphore_signal(barrier, inc=1, device_id=(device,), device_id_type=MESH)

    for peer in peers:
        greet(peer)
    greet(in_row(1))
    greet(in_row(ROW - 1))

    loads = [
        pltpu.make_async_copy(src, dst, load_sem.at[i])
        for i, (src, dst) in enumerate(
            (
                (sends_hbm, sends_ref),
                (x_hbm, x_ref),
                (nb_hbm, nb_ref),
                (lw_hbm, lw_ref),
                (ct_hbm, ct_ref),
                (w_hbm, w_ref),
            )
        )
    ]
    for load in loads:
        load.start()

    @pl.loop(2, rows - 1)
    def _(step):
        greet(in_column(step))

    @pl.loop(2, ROW - 1)
    def _(step):
        greet(in_row(step))

    lane_low = lax.broadcasted_iota(jnp.int32, (CH // 2, 128), 1) < HALO

    def halo_copy(chain, step, place):
        return pltpu.make_async_remote_copy(
            src_ref=outgoing.at[chain, step, place],
            dst_ref=incoming.at[chain, step, place],
            send_sem=halo_send.at[chain, step],
            recv_sem=halo_recv.at[chain, step],
            device_id=(peers[place if chain == 0 else place ^ 1],),
            device_id_type=MESH,
        )

    def halo_all(chain, step):
        return pltpu.make_async_remote_copy(
            src_ref=outgoing.at[chain, step],
            dst_ref=incoming.at[chain, step],
            send_sem=halo_send.at[chain, step],
            recv_sem=halo_recv.at[chain, step],
            device_id=(peers[0],),
            device_id_type=MESH,
        )

    def post(chain, step, columns, start=True):
        for pair in range(PEERS // 2):
            block = columns[:, 128 * pair : 128 * pair + 128]
            upper, lower = block[: CH // 2], block[CH // 2 :]
            outgoing[chain, step, 2 * pair] = jnp.where(lane_low, upper, turned(lower))
            outgoing[chain, step, 2 * pair + 1] = jnp.where(lane_low, turned(upper), lower)
            if start:
                halo_copy(chain, step, 2 * pair).start()
                halo_copy(chain, step, 2 * pair + 1).start()

    def collect(chain, step):
        halo_all(chain, step).wait_recv()
        blocks = []
        for pair in range(PEERS // 2):
            one, two = incoming[chain, step, 2 * pair], incoming[chain, step, 2 * pair + 1]
            blocks.append(
                jnp.concatenate(
                    [jnp.where(lane_low, one, turned(two)), jnp.where(lane_low, turned(one), two)],
                    axis=0,
                )
            )
        return jnp.concatenate(blocks, axis=1)

    loads[0].wait()
    pixel = lax.broadcasted_iota(jnp.int32, (PIX, 128), 0)
    for pair in range(PEERS // 2):
        listed = jnp.concatenate(
            [sends_ref[ORDER[2 * pair + i] : ORDER[2 * pair + i] + 1, :] for i in range(2)], axis=1
        )
        s_mat[:, 128 * pair : 128 * pair + 128] = jnp.where(pixel == listed, 1.0, 0.0).astype(BF16)
    loads[1].wait()
    xs = [x_ref[...].astype(F32)]
    post(0, 0, dot(x_ref[...], s_mat[...]), start=False)
    loads[2].wait()
    slot = lax.broadcasted_iota(jnp.int32, (HALO, PIX), 0) + PIX
    for place, o in enumerate(ORDER):
        hit = slot + HALO * o == nb_ref[o + 1 : o + 2, :]
        t_mat[HALO * place : HALO * place + HALO, :] = jnp.where(hit, 1.0, 0.0).astype(BF16)
    loads[3].wait()
    lists = jnp.concatenate([lw_ref[o + 1 : o + 2, :] for o in ORDER], axis=0)
    high, rest = split(lists)
    middle = (lists - high.astype(F32)).astype(BF16)
    low = (lists - high.astype(F32) - middle.astype(F32)).astype(BF16)
    found = dot_nt(jnp.concatenate([high, middle, low], axis=0), t_mat[...])
    found = found[:PEERS] + found[PEERS : 2 * PEERS] + found[2 * PEERS :]
    own = lax.broadcasted_iota(jnp.int32, (PEERS, LISTED), 1) // HALO
    own = own == lax.broadcasted_iota(jnp.int32, (PEERS, LISTED), 0)
    list_weight = jnp.sum(jnp.where(own, found, 0.0), axis=0, keepdims=True)
    loads[4].wait()
    cs = [ct_ref[...].astype(F32)]
    post(1, 0, dot_nt(ct_ref[...], t_mat[...]) * list_weight, start=False)
    pl.semaphore_wait(barrier, PEERS + ROW - 1 + rows - 3)
    for chain in range(2):
        for place in range(PEERS):
            halo_copy(chain, 0, place).start()

    for base in range(0, PIX, 32):
        column = lax.broadcasted_iota(jnp.int32, (32, PIX), 0) + base
        block = jnp.zeros((32, PIX), F32)
        for entry in range(STENCIL):
            block = block + jnp.where(
                column == nb_ref[entry : entry + 1, :], lw_ref[entry : entry + 1, :], 0.0
            )
        high, low = split(block)
        a_high[base : base + 32, :] = high
        a_low[base : base + 32, :] = low
    loads[5].wait()

    def near(value, times):
        return product(value, a_high[...], times) + times(value.astype(BF16), a_low[...])

    def out_term(k):
        return dot_tn(w_ref[CH * k : CH * k + CH, :], xs[k].astype(BF16))

    def mg_term(k):
        high, low = split(cs[k])
        weight = w_ref[CH * k : CH * k + CH, :]
        return dot(weight, high) + dot(weight, low)

    def inner(x, c):
        x_high, x_low = split(x)
        c_high, c_low = split(c)
        both = dot_nt(jnp.concatenate([x_high, x_low], axis=0), c_high)
        return both[:CH] + both[CH:] + dot_nt(x_high, c_low)

    class Batch:
        def __init__(self, which):
            self.which = which
            self.sums, self.row_in, self.part, self.column_in, self.total = sum_refs[
                5 * which : 5 * which + 5
            ]

        def copy(self, stage, src, dst, device):
            return pltpu.make_async_remote_copy(
                src_ref=src,
                dst_ref=dst,
                send_sem=sum_send.at[self.which, stage],
                recv_sem=sum_recv.at[self.which, stage],
                device_id=(device,),
                device_id_type=MESH,
            )

        def all_of(self, stage):
            ref = (self.row_in, self.column_in, self.total)[stage]
            ref = ref.at[pl.ds(0, (ROW, rows, ROW)[stage] - 1)]
            return self.copy(stage, ref, ref, peers[0])

        def start(self, blocks):
            at = 0
            for block in blocks:
                n = block.shape[0] // ROW
                for i in range(ROW):
                    self.sums[i, at : at + n, :] = block[n * i : n * i + n]
                at += n

            @pl.loop(1, ROW)
            def _(i):
                other = (my_column + i) % ROW
                self.copy(
                    0, self.sums.at[other], self.row_in.at[my_column], my_row * ROW + other
                ).start()

            self.row_in[my_column] = self.sums[my_column]

        def across(self):
            self.all_of(0).wait_recv()
            piece = self.row_in[0]
            for i in range(1, ROW):
                piece = piece + self.row_in[i]
            self.part[...] = piece

            @pl.loop(1, rows)
            def _(i):
                self.copy(1, self.part, self.column_in.at[my_row], in_column(i)).start()

            self.column_in[my_row] = piece

        def back(self):
            self.all_of(1).wait_recv()
            piece = self.column_in[0]
            for i in range(1, rows):
                piece = piece + self.column_in[i]
            self.total[my_column] = piece

            @pl.loop(1, ROW)
            def _(i):
                mine = self.total.at[my_column]
                self.copy(2, mine, mine, in_row(i)).start()

        def arrive(self):
            self.all_of(2).wait_recv()

        def end(self):
            for stage in range(3):
                self.all_of(stage).wait_send()

    early, late = Batch(0), Batch(1)
    scale = 1.0 / math.sqrt(count * PIX)

    def halves(value):
        return jnp.concatenate([value[: CH // 2], value[CH // 2 :]], axis=1)

    out_sum = mg_sum = None
    for step in range(STEPS):
        x_near = near(xs[step], dot)
        c_near = near(cs[step], dot_nt)
        if step == 2:
            late.across()
        if step == 3:
            late.back()
            early.back()
        x_next = x_near + product(collect(0, step) * list_weight, t_mat[...], dot)
        if step:
            x_next = 2.0 * x_next - xs[step - 1]
        xs.append(x_next)
        if step in (0, 2):
            post(0, step + 1, product(x_next, s_mat[...], dot))
        c_next = c_near + product(collect(1, step), s_mat[...], dot_nt)
        if step:
            c_next = 2.0 * c_next - cs[step - 1]
        cs.append(c_next)
        if step == 1:
            last = inner(xs[2], jnp.concatenate([cs[1], cs[2]], axis=0)) * (2.0 * scale)
            late.start([last - jnp.concatenate([p1, p0], axis=1)])
            post(0, step + 1, product(x_next, s_mat[...], dot))
        if step + 1 < STEPS:
            post(1, step + 1, product(c_next, t_mat[...], dot_nt) * list_weight)
        if step == 0:
            p0 = dot_nt(x_ref[...], ct_ref[...]) * scale
            p1 = dot_nt(xs[1].astype(BF16), ct_ref[...]) * scale
            p2 = inner(xs[1], cs[1]) * (2.0 * scale) - p0
            early.start([jnp.concatenate([p0, p1], axis=1), halves(p2)])
        if step == 1:
            early.across()
        if step < STEPS - 1:
            term_out, term_mg = out_term(step), mg_term(step)
            out_sum = term_out if out_sum is None else out_sum + term_out
            mg_sum = term_mg if mg_sum is None else mg_sum + term_mg

    for k in (STEPS - 1, STEPS):
        out_sum = out_sum + out_term(k)
        mg_sum = mg_sum + mg_term(k)
    out_ref[...] = out_sum.astype(BF16)
    mg_ref[...] = mg_sum.astype(BF16)
    early.arrive()

    def rows_of(batch, lower, upper):
        return jnp.concatenate([batch.total[i, lower:upper, :] for i in range(ROW)], axis=0)

    first = rows_of(early, 0, 4)
    third = rows_of(early, 4, 6)
    wg_ref[0] = first[:, :CH]
    wg_ref[1] = first[:, CH:]
    wg_ref[2, : CH // 2] = third[:, :CH]
    wg_ref[2, CH // 2 :] = third[:, CH:]
    for chain in range(2):
        for step in range(STEPS):
            halo_all(chain, step).wait_send()
    early.end()
    late.arrive()
    second = rows_of(late, 0, 4)
    wg_ref[3] = second[:, :CH]
    wg_ref[4] = second[:, CH:]
    late.end()


def store_results(out_ref, mg_ref, wg_ref, out_hbm, mg_hbm, wg_hbm, sem):
    copies = [
        pltpu.make_async_copy(src, dst, sem.at[i])
        for i, (src, dst) in enumerate(((wg_ref, wg_hbm), (out_ref, out_hbm), (mg_ref, mg_hbm)))
    ]
    for copy in copies:
        copy.start()
    for copy in copies:
        copy.wait()


def solution(mesh):
    count = mesh.shape["pix"]
    rows = count // ROW
    dma = pltpu.SemaphoreType.DMA

    def local(input_maps, cheb_weights, cotangent, neighbours, lap_weights, send_rows):
        def body(*refs):
            kernel(count, *refs)

        results = pl.pallas_call(
            body,
            out_shape=(
                pltpu.VMEM((CH, PIX), BF16),
                pltpu.VMEM((CH, PIX), BF16),
                pltpu.VMEM((KTERMS, CH, CH), F32),
            ),
            in_specs=[pl.BlockSpec(memory_space=pltpu.HBM)] * 6,
            out_specs=tuple([pl.BlockSpec(memory_space=pltpu.VMEM)] * 3),
            scratch_shapes=[
                pltpu.VMEM((CH, PIX), BF16),
                pltpu.VMEM((KTERMS * CH, CH), BF16),
                pltpu.VMEM((CH, PIX), BF16),
                pltpu.VMEM((STENCIL, PIX), jnp.int32),
                pltpu.VMEM((STENCIL, PIX), F32),
                pltpu.VMEM((PEERS, HALO), jnp.int32),
                dma((6,)),
                pltpu.VMEM((PIX, PIX), BF16),
                pltpu.VMEM((PIX, PIX), BF16),
                pltpu.VMEM((PIX, LISTED), BF16),
                pltpu.VMEM((LISTED, PIX), BF16),
                pltpu.VMEM((2, STEPS, PEERS, CH // 2, 128), F32),
                pltpu.VMEM((2, STEPS, PEERS, CH // 2, 128), F32),
                dma((2, STEPS)),
                dma((2, STEPS)),
                dma((2, 3)),
                dma((2, 3)),
                *[
                    pltpu.VMEM(lead + (share, 128), F32)
                    for share in SHARES
                    for lead in ((ROW,), (ROW,), (), (rows,), (ROW,))
                ],
            ],
            compiler_params=pltpu.CompilerParams(
                collective_id=0, has_side_effects=True, vmem_limit_bytes=16 * 1024 * 1024
            ),
        )(
            *[
                pltpu.with_memory_space_constraint(operand, pltpu.HBM)
                for operand in (
                    input_maps,
                    cheb_weights.reshape(KTERMS * CH, CH),
                    cotangent,
                    neighbours,
                    lap_weights,
                    send_rows,
                )
            ]
        )
        return pl.pallas_call(
            store_results,
            out_shape=tuple(jax.ShapeDtypeStruct(r.shape, r.dtype) for r in results),
            in_specs=[pl.BlockSpec(memory_space=pltpu.VMEM)] * 3,
            out_specs=tuple([pl.BlockSpec(memory_space=pltpu.HBM)] * 3),
            scratch_shapes=[dma((3,))],
        )(*[pltpu.with_memory_space_constraint(r, pltpu.VMEM) for r in results])

    return jax.shard_map(
        local,
        mesh=mesh,
        in_specs=(
            P(None, "pix"),
            P(),
            P(None, "pix"),
            P(None, "pix"),
            P(None, "pix"),
            P("pix", None),
        ),
        out_specs=(P(None, "pix"), P(None, "pix"), P()),
        check_vma=False,
    )
```

```python
import math

import jax
import jax.numpy as jnp
from jax import lax
from jax.experimental import pallas as pl
from jax.experimental.pallas import tpu as pltpu
from jax.sharding import PartitionSpec as P

CH = 64
KTERMS = 5
PIX = 256
HALO = 64
ROW = 16
PEERS = 8
STENCIL = 9
STEPS = KTERMS - 1
OFFSETS = [1, -1, 16, -16, 17, 15, -15, -17]
ORDER = [0, 1, 2, 3, 4, 7, 5, 6]
LISTED = PEERS * HALO
SHARES = [6, 4]
MESH = pl.DeviceIdType.MESH
F32 = jnp.float32
BF16 = jnp.bfloat16


def split(value):
    high = value.astype(BF16)
    return high, (value - high.astype(F32)).astype(BF16)


def dot(a, b):
    return jnp.dot(a, b, preferred_element_type=F32)


def dot_nt(a, b):
    return lax.dot_general(a, b, (((1,), (1,)), ((), ())), preferred_element_type=F32)


def dot_tn(a, b):
    return lax.dot_general(a, b, (((0,), (0,)), ((), ())), preferred_element_type=F32)


def product(value, matrix, times):
    high, low = split(value)
    both = times(jnp.concatenate([high, low], axis=0), matrix)
    rows = value.shape[0]
    return both[:rows] + both[rows:]


def turned(value):
    return pltpu.roll(value, HALO, 1)


def kernel(
    count,
    x_hbm,
    w_hbm,
    ct_hbm,
    nb_hbm,
    lw_hbm,
    sends_hbm,
    out_ref,
    mg_ref,
    wg_ref,
    x_ref,
    w_ref,
    ct_ref,
    nb_ref,
    lw_ref,
    sends_ref,
    load_sem,
    known,
    a_high,
    a_low,
    s_mat,
    t_mat,
    outgoing,
    incoming,
    halo_send,
    halo_recv,
    sum_send,
    sum_recv,
    *sum_refs,
):
    me = lax.axis_index("pix")
    rows = count // ROW
    my_row, my_column = me // ROW, me % ROW
    peers = [(me + OFFSETS[o] + count) % count for o in ORDER]

    def in_row(step):
        return my_row * ROW + (my_column + step) % ROW

    def in_column(step):
        return (my_row + step) % rows * ROW + my_column

    barrier = pltpu.get_barrier_semaphore()

    def greet(device):
        pl.semaphore_signal(barrier, inc=1, device_id=(device,), device_id_type=MESH)

    for peer in peers:
        greet(peer)
    for step in (1, ROW - 1):
        greet(in_row(step))

    loads = [
        pltpu.make_async_copy(src, dst, load_sem.at[i])
        for i, (src, dst) in enumerate(
            (
                (sends_hbm, sends_ref),
                (x_hbm, x_ref),
                (nb_hbm, nb_ref),
                (lw_hbm, lw_ref),
                (ct_hbm, ct_ref),
                (w_hbm, w_ref),
            )
        )
    ]
    for load in loads:
        load.start()

    def spread(k):
        for ring, size in ((in_row, ROW), (in_column, rows)):
            if 4 * 2**k <= size:
                for other in (2**k, size - 2**k):
                    pl.semaphore_signal(
                        known.at[k], inc=1, device_id=(ring(other),), device_id_type=MESH
                    )

    def heard(k):
        pl.semaphore_wait(known.at[k], sum(2 for size in (ROW, rows) if 4 * 2**k <= size))

    lane_low = lax.broadcasted_iota(jnp.int32, (CH // 2, 128), 1) < HALO

    def halo_copy(chain, step, place):
        return pltpu.make_async_remote_copy(
            src_ref=outgoing.at[chain, step, place],
            dst_ref=incoming.at[chain, step, place],
            send_sem=halo_send.at[chain, step],
            recv_sem=halo_recv.at[chain, step],
            device_id=(peers[place if chain == 0 else place ^ 1],),
            device_id_type=MESH,
        )

    def halo_all(chain, step):
        return pltpu.make_async_remote_copy(
            src_ref=outgoing.at[chain, step],
            dst_ref=incoming.at[chain, step],
            send_sem=halo_send.at[chain, step],
            recv_sem=halo_recv.at[chain, step],
            device_id=(peers[0],),
            device_id_type=MESH,
        )

    def post(chain, step, columns, start=True):
        for pair in range(PEERS // 2):
            block = columns[:, 128 * pair : 128 * pair + 128]
            upper, lower = block[: CH // 2], block[CH // 2 :]
            outgoing[chain, step, 2 * pair] = jnp.where(lane_low, upper, turned(lower))
            outgoing[chain, step, 2 * pair + 1] = jnp.where(lane_low, turned(upper), lower)
            if start:
                halo_copy(chain, step, 2 * pair).start()
                halo_copy(chain, step, 2 * pair + 1).start()

    def collect(chain, step):
        halo_all(chain, step).wait_recv()
        blocks = []
        for pair in range(PEERS // 2):
            one, two = incoming[chain, step, 2 * pair], incoming[chain, step, 2 * pair + 1]
            blocks.append(
                jnp.concatenate(
                    [jnp.where(lane_low, one, turned(two)), jnp.where(lane_low, turned(one), two)],
                    axis=0,
                )
            )
        return jnp.concatenate(blocks, axis=1)

    loads[0].wait()
    pixel = lax.broadcasted_iota(jnp.int32, (PIX, 128), 0)
    for pair in range(PEERS // 2):
        listed = jnp.concatenate(
            [sends_ref[ORDER[2 * pair + i] : ORDER[2 * pair + i] + 1, :] for i in range(2)], axis=1
        )
        s_mat[:, 128 * pair : 128 * pair + 128] = jnp.where(pixel == listed, 1.0, 0.0).astype(BF16)
    loads[1].wait()
    xs = [x_ref[...].astype(F32)]
    post(0, 0, dot(x_ref[...], s_mat[...]), start=False)
    loads[2].wait()
    slot = lax.broadcasted_iota(jnp.int32, (HALO, PIX), 0) + PIX
    for place, o in enumerate(ORDER):
        hit = slot + HALO * o == nb_ref[o + 1 : o + 2, :]
        t_mat[HALO * place : HALO * place + HALO, :] = jnp.where(hit, 1.0, 0.0).astype(BF16)
    loads[3].wait()
    lists = jnp.concatenate([lw_ref[o + 1 : o + 2, :] for o in ORDER], axis=0)
    high, rest = split(lists)
    middle = (lists - high.astype(F32)).astype(BF16)
    low = (lists - high.astype(F32) - middle.astype(F32)).astype(BF16)
    found = dot_nt(jnp.concatenate([high, middle, low], axis=0), t_mat[...])
    found = found[:PEERS] + found[PEERS : 2 * PEERS] + found[2 * PEERS :]
    own = lax.broadcasted_iota(jnp.int32, (PEERS, LISTED), 1) // HALO
    own = own == lax.broadcasted_iota(jnp.int32, (PEERS, LISTED), 0)
    list_weight = jnp.sum(jnp.where(own, found, 0.0), axis=0, keepdims=True)
    loads[4].wait()
    cs = [ct_ref[...].astype(F32)]
    post(1, 0, dot_nt(ct_ref[...], t_mat[...]) * list_weight, start=False)
    pl.semaphore_wait(barrier, PEERS + 2)
    for chain in range(2):
        for place in range(PEERS):
            halo_copy(chain, 0, place).start()
    spread(0)

    for base in range(0, PIX, 32):
        column = lax.broadcasted_iota(jnp.int32, (32, PIX), 0) + base
        block = jnp.zeros((32, PIX), F32)
        for entry in range(STENCIL):
            block = block + jnp.where(
                column == nb_ref[entry : entry + 1, :], lw_ref[entry : entry + 1, :], 0.0
            )
        high, low = split(block)
        a_high[base : base + 32, :] = high
        a_low[base : base + 32, :] = low
    loads[5].wait()

    def near(value, times):
        return product(value, a_high[...], times) + times(value.astype(BF16), a_low[...])

    def out_term(k):
        return dot_tn(w_ref[CH * k : CH * k + CH, :], xs[k].astype(BF16))

    def mg_term(k):
        high, low = split(cs[k])
        weight = w_ref[CH * k : CH * k + CH, :]
        return dot(weight, high) + dot(weight, low)

    def inner(x, c):
        x_high, x_low = split(x)
        c_high, c_low = split(c)
        both = dot_nt(jnp.concatenate([x_high, x_low], axis=0), c_high)
        return both[:CH] + both[CH:] + dot_nt(x_high, c_low)

    class Batch:
        def __init__(self, which):
            self.which = which
            self.sums, self.row_in, self.part, self.column_in, self.total = sum_refs[
                5 * which : 5 * which + 5
            ]

        def copy(self, stage, src, dst, device):
            return pltpu.make_async_remote_copy(
                src_ref=src,
                dst_ref=dst,
                send_sem=sum_send.at[self.which, stage],
                recv_sem=sum_recv.at[self.which, stage],
                device_id=(device,),
                device_id_type=MESH,
            )

        def all_of(self, stage):
            ref = (self.row_in, self.column_in, self.total)[stage]
            ref = ref.at[pl.ds(0, (ROW, rows, ROW)[stage] - 1)]
            return self.copy(stage, ref, ref, peers[0])

        def start(self, blocks):
            at = 0
            for block in blocks:
                n = block.shape[0] // ROW
                for i in range(ROW):
                    self.sums[i, at : at + n, :] = block[n * i : n * i + n]
                at += n

            @pl.loop(1, ROW)
            def _(i):
                other = (my_column + i) % ROW
                self.copy(
                    0, self.sums.at[other], self.row_in.at[my_column], my_row * ROW + other
                ).start()

            self.row_in[my_column] = self.sums[my_column]

        def across(self):
            self.all_of(0).wait_recv()
            piece = self.row_in[0]
            for i in range(1, ROW):
                piece = piece + self.row_in[i]
            self.part[...] = piece

            @pl.loop(1, rows)
            def _(i):
                self.copy(1, self.part, self.column_in.at[my_row], in_column(i)).start()

            self.column_in[my_row] = piece

        def back(self):
            self.all_of(1).wait_recv()
            piece = self.column_in[0]
            for i in range(1, rows):
                piece = piece + self.column_in[i]
            self.total[my_column] = piece

            @pl.loop(1, ROW)
            def _(i):
                mine = self.total.at[my_column]
                self.copy(2, mine, mine, in_row(i)).start()

        def arrive(self):
            self.all_of(2).wait_recv()

        def end(self):
            for stage in range(3):
                self.all_of(stage).wait_send()

    early, late = Batch(0), Batch(1)
    scale = 1.0 / math.sqrt(count * PIX)

    def halves(value):
        return jnp.concatenate([value[: CH // 2], value[CH // 2 :]], axis=1)

    out_sum = mg_sum = None
    for step in range(STEPS):
        x_near = near(xs[step], dot)
        c_near = near(cs[step], dot_nt)
        if step == 2:
            late.across()
        if step == 3:
            late.back()
            early.back()
        if step == 0:
            heard(0)
            spread(1)
            heard(1)
            spread(2)
        x_next = x_near + product(collect(0, step) * list_weight, t_mat[...], dot)
        if step:
            x_next = 2.0 * x_next - xs[step - 1]
        xs.append(x_next)
        if step + 1 < STEPS:
            listed = product(x_next, s_mat[...], dot)
        if step in (0, 2):
            post(0, step + 1, listed)
        if step == 1:
            none = jnp.zeros((CH, PIX), F32)
            last = inner(x_next, jnp.concatenate([cs[1], none], axis=0)) - half_early
        c_next = c_near + product(collect(1, step), s_mat[...], dot_nt)
        if step:
            c_next = 2.0 * c_next - cs[step - 1]
        cs.append(c_next)
        if step == 1:
            last = last + inner(x_next, jnp.concatenate([none, c_next], axis=0))
            late.start([last * (2.0 * scale)])
            post(0, step + 1, listed)
        if step + 1 < STEPS:
            post(1, step + 1, product(c_next, t_mat[...], dot_nt) * list_weight)
        if step == 0:
            heard(2)
            spread(3)
            p0 = dot_nt(x_ref[...], ct_ref[...])
            p1 = dot_nt(xs[1].astype(BF16), ct_ref[...])
            p2 = 2.0 * inner(xs[1], cs[1]) - p0
            half_early = 0.5 * jnp.concatenate([p1, p0], axis=1)
            early.start([scale * jnp.concatenate([p0, p1], axis=1), scale * halves(p2)])
        if step == 1:
            heard(3)
            early.across()
        if step < STEPS - 1:
            term_out, term_mg = out_term(step), mg_term(step)
            out_sum = term_out if out_sum is None else out_sum + term_out
            mg_sum = term_mg if mg_sum is None else mg_sum + term_mg

    for k in (STEPS - 1, STEPS):
        out_sum = out_sum + out_term(k)
        mg_sum = mg_sum + mg_term(k)
    out_ref[...] = out_sum.astype(BF16)
    mg_ref[...] = mg_sum.astype(BF16)
    early.arrive()

    def rows_of(batch, lower, upper):
        return jnp.concatenate([batch.total[i, lower:upper, :] for i in range(ROW)], axis=0)

    first = rows_of(early, 0, 4)
    third = rows_of(early, 4, 6)
    wg_ref[0] = first[:, :CH]
    wg_ref[1] = first[:, CH:]
    wg_ref[2, : CH // 2] = third[:, :CH]
    wg_ref[2, CH // 2 :] = third[:, CH:]
    for chain in range(2):
        for step in range(STEPS):
            halo_all(chain, step).wait_send()
    early.end()
    late.arrive()
    second = rows_of(late, 0, 4)
    wg_ref[3] = second[:, :CH]
    wg_ref[4] = second[:, CH:]
    late.end()


def store_results(out_ref, mg_ref, wg_ref, out_hbm, mg_hbm, wg_hbm, sem):
    copies = [
        pltpu.make_async_copy(src, dst, sem.at[i])
        for i, (src, dst) in enumerate(((wg_ref, wg_hbm), (out_ref, out_hbm), (mg_ref, mg_hbm)))
    ]
    for copy in copies:
        copy.start()
    for copy in copies:
        copy.wait()


def solution(mesh):
    count = mesh.shape["pix"]
    rows = count // ROW
    dma = pltpu.SemaphoreType.DMA

    def local(input_maps, cheb_weights, cotangent, neighbours, lap_weights, send_rows):
        def body(*refs):
            kernel(count, *refs)

        results = pl.pallas_call(
            body,
            out_shape=(
                pltpu.VMEM((CH, PIX), BF16),
                pltpu.VMEM((CH, PIX), BF16),
                pltpu.VMEM((KTERMS, CH, CH), F32),
            ),
            in_specs=[pl.BlockSpec(memory_space=pltpu.HBM)] * 6,
            out_specs=tuple([pl.BlockSpec(memory_space=pltpu.VMEM)] * 3),
            scratch_shapes=[
                pltpu.VMEM((CH, PIX), BF16),
                pltpu.VMEM((KTERMS * CH, CH), BF16),
                pltpu.VMEM((CH, PIX), BF16),
                pltpu.VMEM((STENCIL, PIX), jnp.int32),
                pltpu.VMEM((STENCIL, PIX), F32),
                pltpu.VMEM((PEERS, HALO), jnp.int32),
                dma((6,)),
                pltpu.SemaphoreType.REGULAR((4,)),
                pltpu.VMEM((PIX, PIX), BF16),
                pltpu.VMEM((PIX, PIX), BF16),
                pltpu.VMEM((PIX, LISTED), BF16),
                pltpu.VMEM((LISTED, PIX), BF16),
                pltpu.VMEM((2, STEPS, PEERS, CH // 2, 128), F32),
                pltpu.VMEM((2, STEPS, PEERS, CH // 2, 128), F32),
                dma((2, STEPS)),
                dma((2, STEPS)),
                dma((2, 3)),
                dma((2, 3)),
                *[
                    pltpu.VMEM(lead + (share, 128), F32)
                    for share in SHARES
                    for lead in ((ROW,), (ROW,), (), (rows,), (ROW,))
                ],
            ],
            compiler_params=pltpu.CompilerParams(
                collective_id=0, has_side_effects=True, vmem_limit_bytes=16 * 1024 * 1024
            ),
        )(
            *[
                pltpu.with_memory_space_constraint(operand, pltpu.HBM)
                for operand in (
                    input_maps,
                    cheb_weights.reshape(KTERMS * CH, CH),
                    cotangent,
                    neighbours,
                    lap_weights,
                    send_rows,
                )
            ]
        )
        return pl.pallas_call(
            store_results,
            out_shape=tuple(jax.ShapeDtypeStruct(r.shape, r.dtype) for r in results),
            in_specs=[pl.BlockSpec(memory_space=pltpu.VMEM)] * 3,
            out_specs=tuple([pl.BlockSpec(memory_space=pltpu.HBM)] * 3),
            scratch_shapes=[dma((3,))],
        )(*[pltpu.with_memory_space_constraint(r, pltpu.VMEM) for r in results])

    return jax.shard_map(
        local,
        mesh=mesh,
        in_specs=(
            P(None, "pix"),
            P(),
            P(None, "pix"),
            P(None, "pix"),
            P(None, "pix"),
            P("pix", None),
        ),
        out_specs=(P(None, "pix"), P(None, "pix"), P()),
        check_vma=False,
    )
```

```python
import math

import jax
import jax.numpy as jnp
from jax import lax
from jax.experimental import pallas as pl
from jax.experimental.pallas import tpu as pltpu
from jax.sharding import PartitionSpec as P

CH = 64
KTERMS = 5
PIX = 256
HALO = 64
ROW = 16
PEERS = 8
STENCIL = 9
STEPS = KTERMS - 1
OFFSETS = [1, -1, 16, -16, 17, 15, -15, -17]
ORDER = [0, 1, 2, 3, 4, 7, 5, 6]
LISTED = PEERS * HALO
SHARES = [6, 4]
MESH = pl.DeviceIdType.MESH
F32 = jnp.float32
BF16 = jnp.bfloat16


def split(value):
    high = value.astype(BF16)
    return high, (value - high.astype(F32)).astype(BF16)


def dot(a, b):
    return jnp.dot(a, b, preferred_element_type=F32)


def dot_nt(a, b):
    return lax.dot_general(a, b, (((1,), (1,)), ((), ())), preferred_element_type=F32)


def dot_tn(a, b):
    return lax.dot_general(a, b, (((0,), (0,)), ((), ())), preferred_element_type=F32)


def product(value, matrix, times):
    high, low = split(value)
    both = times(jnp.concatenate([high, low], axis=0), matrix)
    rows = value.shape[0]
    return both[:rows] + both[rows:]


def turned(value):
    return pltpu.roll(value, HALO, 1)


def kernel(
    count,
    x_hbm,
    w_hbm,
    ct_hbm,
    nb_hbm,
    lw_hbm,
    sends_hbm,
    out_ref,
    mg_ref,
    wg_ref,
    x_ref,
    w_ref,
    ct_ref,
    nb_ref,
    lw_ref,
    sends_ref,
    load_sem,
    known,
    a_high,
    a_low,
    s_mat,
    t_mat,
    outgoing,
    incoming,
    halo_send,
    halo_recv,
    sum_send,
    sum_recv,
    *sum_refs,
):
    me = lax.axis_index("pix")
    rows = count // ROW
    my_row, my_column = me // ROW, me % ROW
    peers = [(me + OFFSETS[o] + count) % count for o in ORDER]

    def in_row(step):
        return my_row * ROW + (my_column + step) % ROW

    def in_column(step):
        return (my_row + step) % rows * ROW + my_column

    barrier = pltpu.get_barrier_semaphore()

    def greet(device):
        pl.semaphore_signal(barrier, inc=1, device_id=(device,), device_id_type=MESH)

    for peer in peers:
        greet(peer)
    for step in (1, ROW - 1):
        greet(in_row(step))

    loads = [
        pltpu.make_async_copy(src, dst, load_sem.at[i])
        for i, (src, dst) in enumerate(
            (
                (sends_hbm, sends_ref),
                (x_hbm, x_ref),
                (nb_hbm, nb_ref),
                (lw_hbm, lw_ref),
                (ct_hbm, ct_ref),
                (w_hbm, w_ref),
            )
        )
    ]
    for load in loads:
        load.start()

    def spread(k):
        for ring, size in ((in_row, ROW), (in_column, rows)):
            if 4 * 2**k <= size:
                for other in (2**k, size - 2**k):
                    pl.semaphore_signal(
                        known.at[k], inc=1, device_id=(ring(other),), device_id_type=MESH
                    )

    def heard(k):
        pl.semaphore_wait(known.at[k], sum(2 for size in (ROW, rows) if 4 * 2**k <= size))

    lane_low = lax.broadcasted_iota(jnp.int32, (CH // 2, 128), 1) < HALO

    def halo_copy(chain, step, place):
        return pltpu.make_async_remote_copy(
            src_ref=outgoing.at[chain, step, place],
            dst_ref=incoming.at[chain, step, place],
            send_sem=halo_send.at[chain, step],
            recv_sem=halo_recv.at[chain, step],
            device_id=(peers[place if chain == 0 else place ^ 1],),
            device_id_type=MESH,
        )

    def halo_all(chain, step):
        return pltpu.make_async_remote_copy(
            src_ref=outgoing.at[chain, step],
            dst_ref=incoming.at[chain, step],
            send_sem=halo_send.at[chain, step],
            recv_sem=halo_recv.at[chain, step],
            device_id=(peers[0],),
            device_id_type=MESH,
        )

    def post(chain, step, columns, start=True):
        for pair in range(PEERS // 2):
            block = columns[:, 128 * pair : 128 * pair + 128]
            upper, lower = block[: CH // 2], block[CH // 2 :]
            outgoing[chain, step, 2 * pair] = jnp.where(lane_low, upper, turned(lower))
            outgoing[chain, step, 2 * pair + 1] = jnp.where(lane_low, turned(upper), lower)
            if start:
                halo_copy(chain, step, 2 * pair).start()
                halo_copy(chain, step, 2 * pair + 1).start()

    def collect(chain, step):
        halo_all(chain, step).wait_recv()
        blocks = []
        for pair in range(PEERS // 2):
            one, two = incoming[chain, step, 2 * pair], incoming[chain, step, 2 * pair + 1]
            blocks.append(
                jnp.concatenate(
                    [jnp.where(lane_low, one, turned(two)), jnp.where(lane_low, turned(one), two)],
                    axis=0,
                )
            )
        return jnp.concatenate(blocks, axis=1)

    loads[0].wait()
    pixel = lax.broadcasted_iota(jnp.int32, (PIX, 128), 0)
    for pair in range(PEERS // 2):
        listed = jnp.concatenate(
            [sends_ref[ORDER[2 * pair + i] : ORDER[2 * pair + i] + 1, :] for i in range(2)], axis=1
        )
        s_mat[:, 128 * pair : 128 * pair + 128] = jnp.where(pixel == listed, 1.0, 0.0).astype(BF16)
    loads[1].wait()
    xs = [x_ref[...].astype(F32)]
    post(0, 0, dot(x_ref[...], s_mat[...]), start=False)
    loads[2].wait()
    slot = lax.broadcasted_iota(jnp.int32, (HALO, PIX), 0) + PIX
    for place, o in enumerate(ORDER):
        hit = slot + HALO * o == nb_ref[o + 1 : o + 2, :]
        t_mat[HALO * place : HALO * place + HALO, :] = jnp.where(hit, 1.0, 0.0).astype(BF16)
    loads[3].wait()
    lists = jnp.concatenate([lw_ref[o + 1 : o + 2, :] for o in ORDER], axis=0)
    high, rest = split(lists)
    middle = (lists - high.astype(F32)).astype(BF16)
    low = (lists - high.astype(F32) - middle.astype(F32)).astype(BF16)
    found = dot_nt(jnp.concatenate([high, middle, low], axis=0), t_mat[...])
    found = found[:PEERS] + found[PEERS : 2 * PEERS] + found[2 * PEERS :]
    own = lax.broadcasted_iota(jnp.int32, (PEERS, LISTED), 1) // HALO
    own = own == lax.broadcasted_iota(jnp.int32, (PEERS, LISTED), 0)
    list_weight = jnp.sum(jnp.where(own, found, 0.0), axis=0, keepdims=True)
    loads[4].wait()
    cs = [ct_ref[...].astype(F32)]
    post(1, 0, dot_nt(ct_ref[...], t_mat[...]) * list_weight, start=False)
    pl.semaphore_wait(barrier, PEERS + 2)
    for chain in range(2):
        for place in range(PEERS):
            halo_copy(chain, 0, place).start()
    spread(0)

    for base in range(0, PIX, 32):
        column = lax.broadcasted_iota(jnp.int32, (32, PIX), 0) + base
        block = jnp.zeros((32, PIX), F32)
        for entry in range(STENCIL):
            block = block + jnp.where(
                column == nb_ref[entry : entry + 1, :], lw_ref[entry : entry + 1, :], 0.0
            )
        high, low = split(block)
        a_high[base : base + 32, :] = high
        a_low[base : base + 32, :] = low
    loads[5].wait()

    def near(value, times):
        return product(value, a_high[...], times) + times(value.astype(BF16), a_low[...])

    def out_term(k):
        return dot_tn(w_ref[CH * k : CH * k + CH, :], xs[k].astype(BF16))

    def mg_term(k):
        high, low = split(cs[k])
        weight = w_ref[CH * k : CH * k + CH, :]
        return dot(weight, high) + dot(weight, low)

    def inner(x, c):
        x_high, x_low = split(x)
        c_high, c_low = split(c)
        both = dot_nt(jnp.concatenate([x_high, x_low], axis=0), c_high)
        return both[:CH] + both[CH:] + dot_nt(x_high, c_low)

    class Batch:
        def __init__(self, which):
            self.which = which
            self.sums, self.row_in, self.part, self.column_in, self.total = sum_refs[
                5 * which : 5 * which + 5
            ]

        def copy(self, stage, src, dst, device):
            return pltpu.make_async_remote_copy(
                src_ref=src,
                dst_ref=dst,
                send_sem=sum_send.at[self.which, stage],
                recv_sem=sum_recv.at[self.which, stage],
                device_id=(device,),
                device_id_type=MESH,
            )

        def all_of(self, stage):
            ref = (self.row_in, self.column_in, self.total)[stage]
            ref = ref.at[pl.ds(0, (ROW, rows, ROW)[stage] - 1)]
            return self.copy(stage, ref, ref, peers[0])

        def start(self, blocks):
            at = 0
            for block in blocks:
                n = block.shape[0] // ROW
                for i in range(ROW):
                    self.sums[i, at : at + n, :] = block[n * i : n * i + n]
                at += n

            @pl.loop(1, ROW)
            def _(i):
                other = (my_column + i) % ROW
                self.copy(
                    0, self.sums.at[other], self.row_in.at[my_column], my_row * ROW + other
                ).start()

            self.row_in[my_column] = self.sums[my_column]

        def across(self):
            self.all_of(0).wait_recv()
            piece = self.row_in[0]
            for i in range(1, ROW):
                piece = piece + self.row_in[i]
            self.part[...] = piece

            @pl.loop(1, rows)
            def _(i):
                self.copy(1, self.part, self.column_in.at[my_row], in_column(i)).start()

            self.column_in[my_row] = piece

        def back(self):
            self.all_of(1).wait_recv()
            piece = self.column_in[0]
            for i in range(1, rows):
                piece = piece + self.column_in[i]
            self.total[my_column] = piece

            @pl.loop(1, ROW)
            def _(i):
                mine = self.total.at[my_column]
                self.copy(2, mine, mine, in_row(i)).start()

        def arrive(self):
            self.all_of(2).wait_recv()

        def end(self):
            for stage in range(3):
                self.all_of(stage).wait_send()

    early, late = Batch(0), Batch(1)
    scale = 1.0 / math.sqrt(count * PIX)

    def halves(value):
        return jnp.concatenate([value[: CH // 2], value[CH // 2 :]], axis=1)

    out_sum = mg_sum = None
    for step in range(STEPS):
        x_near = near(xs[step], dot)
        c_near = near(cs[step], dot_nt)
        if step == 2:
            late.across()
        if step == 3:
            early.back()
            late.back()
        if step == 0:
            heard(0)
            spread(1)
            heard(1)
            spread(2)
        x_next = x_near + product(collect(0, step) * list_weight, t_mat[...], dot)
        if step:
            x_next = 2.0 * x_next - xs[step - 1]
        xs.append(x_next)
        if step + 1 < STEPS:
            listed = product(x_next, s_mat[...], dot)
        if step in (0, 2):
            post(0, step + 1, listed)
        if step == 1:
            none = jnp.zeros((CH, PIX), F32)
            last = inner(x_next, jnp.concatenate([cs[1], none], axis=0)) - half_early
        c_next = c_near + product(collect(1, step), s_mat[...], dot_nt)
        if step:
            c_next = 2.0 * c_next - cs[step - 1]
        cs.append(c_next)
        if step == 1:
            last = last + inner(x_next, jnp.concatenate([none, c_next], axis=0))
            late.start([last * (2.0 * scale)])
            post(0, step + 1, listed)
        if step + 1 < STEPS:
            post(1, step + 1, product(c_next, t_mat[...], dot_nt) * list_weight)
        if step == 0:
            heard(2)
            spread(3)
            p0 = dot_nt(x_ref[...], ct_ref[...])
            p1 = dot_nt(xs[1].astype(BF16), ct_ref[...])
            p2 = 2.0 * inner(xs[1], cs[1]) - p0
            half_early = 0.5 * jnp.concatenate([p1, p0], axis=1)
            early.start([scale * jnp.concatenate([p0, p1], axis=1), scale * halves(p2)])
        if step == 1:
            heard(3)
            early.across()
        if step < STEPS - 1:
            term_out, term_mg = out_term(step), mg_term(step)
            out_sum = term_out if out_sum is None else out_sum + term_out
            mg_sum = term_mg if mg_sum is None else mg_sum + term_mg

    for k in (STEPS - 1, STEPS):
        out_sum = out_sum + out_term(k)
        mg_sum = mg_sum + mg_term(k)
    out_ref[...] = out_sum.astype(BF16)
    mg_ref[...] = mg_sum.astype(BF16)
    early.arrive()

    def rows_of(batch, lower, upper):
        return jnp.concatenate([batch.total[i, lower:upper, :] for i in range(ROW)], axis=0)

    first = rows_of(early, 0, 4)
    third = rows_of(early, 4, 6)
    wg_ref[0] = first[:, :CH]
    wg_ref[1] = first[:, CH:]
    wg_ref[2, : CH // 2] = third[:, :CH]
    wg_ref[2, CH // 2 :] = third[:, CH:]
    for chain in range(2):
        for step in range(STEPS):
            halo_all(chain, step).wait_send()
    early.end()
    late.arrive()
    second = rows_of(late, 0, 4)
    wg_ref[3] = second[:, :CH]
    wg_ref[4] = second[:, CH:]
    late.end()


def store_results(out_ref, mg_ref, wg_ref, out_hbm, mg_hbm, wg_hbm, sem):
    copies = [
        pltpu.make_async_copy(src, dst, sem.at[i])
        for i, (src, dst) in enumerate(((wg_ref, wg_hbm), (out_ref, out_hbm), (mg_ref, mg_hbm)))
    ]
    for copy in copies:
        copy.start()
    for copy in copies:
        copy.wait()


def solution(mesh):
    count = mesh.shape["pix"]
    rows = count // ROW
    dma = pltpu.SemaphoreType.DMA

    def local(input_maps, cheb_weights, cotangent, neighbours, lap_weights, send_rows):
        def body(*refs):
            kernel(count, *refs)

        results = pl.pallas_call(
            body,
            out_shape=(
                pltpu.VMEM((CH, PIX), BF16),
                pltpu.VMEM((CH, PIX), BF16),
                pltpu.VMEM((KTERMS, CH, CH), F32),
            ),
            in_specs=[pl.BlockSpec(memory_space=pltpu.HBM)] * 6,
            out_specs=tuple([pl.BlockSpec(memory_space=pltpu.VMEM)] * 3),
            scratch_shapes=[
                pltpu.VMEM((CH, PIX), BF16),
                pltpu.VMEM((KTERMS * CH, CH), BF16),
                pltpu.VMEM((CH, PIX), BF16),
                pltpu.VMEM((STENCIL, PIX), jnp.int32),
                pltpu.VMEM((STENCIL, PIX), F32),
                pltpu.VMEM((PEERS, HALO), jnp.int32),
                dma((6,)),
                pltpu.SemaphoreType.REGULAR((4,)),
                pltpu.VMEM((PIX, PIX), BF16),
                pltpu.VMEM((PIX, PIX), BF16),
                pltpu.VMEM((PIX, LISTED), BF16),
                pltpu.VMEM((LISTED, PIX), BF16),
                pltpu.VMEM((2, STEPS, PEERS, CH // 2, 128), F32),
                pltpu.VMEM((2, STEPS, PEERS, CH // 2, 128), F32),
                dma((2, STEPS)),
                dma((2, STEPS)),
                dma((2, 3)),
                dma((2, 3)),
                *[
                    pltpu.VMEM(lead + (share, 128), F32)
                    for share in SHARES
                    for lead in ((ROW,), (ROW,), (), (rows,), (ROW,))
                ],
            ],
            compiler_params=pltpu.CompilerParams(
                collective_id=0, has_side_effects=True, vmem_limit_bytes=16 * 1024 * 1024
            ),
        )(
            *[
                pltpu.with_memory_space_constraint(operand, pltpu.HBM)
                for operand in (
                    input_maps,
                    cheb_weights.reshape(KTERMS * CH, CH),
                    cotangent,
                    neighbours,
                    lap_weights,
                    send_rows,
                )
            ]
        )
        return pl.pallas_call(
            store_results,
            out_shape=tuple(jax.ShapeDtypeStruct(r.shape, r.dtype) for r in results),
            in_specs=[pl.BlockSpec(memory_space=pltpu.VMEM)] * 3,
            out_specs=tuple([pl.BlockSpec(memory_space=pltpu.HBM)] * 3),
            scratch_shapes=[dma((3,))],
        )(*[pltpu.with_memory_space_constraint(r, pltpu.VMEM) for r in results])

    return jax.shard_map(
        local,
        mesh=mesh,
        in_specs=(
            P(None, "pix"),
            P(),
            P(None, "pix"),
            P(None, "pix"),
            P(None, "pix"),
            P("pix", None),
        ),
        out_specs=(P(None, "pix"), P(None, "pix"), P()),
        check_vma=False,
    )
```

```python
import math

import jax
import jax.numpy as jnp
from jax import lax
from jax.experimental import pallas as pl
from jax.experimental.pallas import tpu as pltpu
from jax.sharding import PartitionSpec as P

CH = 64
KTERMS = 5
PIX = 256
HALO = 64
ROW = 16
QUAD, Y_SIZE, Z_SIZE, PLANE = 4, 4, 8, 128
PLACES = 16
PEERS = 8
STENCIL = 9
STEPS = KTERMS - 1
OFFSETS = [1, -1, 16, -16, 17, 15, -15, -17]
ORDER = [0, 1, 2, 3, 4, 7, 5, 6]
LISTED = PEERS * HALO
SHARES = [6, 4]
MESH = pl.DeviceIdType.MESH
F32 = jnp.float32
BF16 = jnp.bfloat16


def split(value):
    high = value.astype(BF16)
    return high, (value - high.astype(F32)).astype(BF16)


def dot(a, b):
    return jnp.dot(a, b, preferred_element_type=F32)


def dot_nt(a, b):
    return lax.dot_general(a, b, (((1,), (1,)), ((), ())), preferred_element_type=F32)


def dot_tn(a, b):
    return lax.dot_general(a, b, (((0,), (0,)), ((), ())), preferred_element_type=F32)


def product(value, matrix, times):
    high, low = split(value)
    both = times(jnp.concatenate([high, low], axis=0), matrix)
    rows = value.shape[0]
    return both[:rows] + both[rows:]


def turned(value):
    return pltpu.roll(value, HALO, 1)


def kernel(
    count,
    x_hbm,
    w_hbm,
    ct_hbm,
    nb_hbm,
    lw_hbm,
    sends_hbm,
    out_ref,
    mg_ref,
    wg_ref,
    x_ref,
    w_ref,
    ct_ref,
    nb_ref,
    lw_ref,
    sends_ref,
    load_sem,
    known,
    a_high,
    a_low,
    s_mat,
    t_mat,
    outgoing,
    incoming,
    halo_send,
    halo_recv,
    sum_send,
    sum_recv,
    *sum_refs,
):
    me = lax.axis_index("pix")
    blocks = count // PLACES
    x_at, z_at, y_at, quad_at = me // PLANE, me // ROW % Z_SIZE, me // QUAD % Y_SIZE, me % QUAD
    my_place, my_block = x_at * QUAD + quad_at, z_at * Y_SIZE + y_at
    peers = [(me + OFFSETS[o] + count) % count for o in ORDER]

    def device_at(place, block):
        return place // QUAD * PLANE + block // Y_SIZE * ROW + block % Y_SIZE * QUAD + place % QUAD

    def in_block(step):
        return device_at((my_place + step) % PLACES, my_block)

    def in_place(step):
        return device_at(my_place, (my_block + step) % blocks)

    def along_z(step):
        return me + ((z_at + step) % Z_SIZE - z_at) * ROW

    def along_y(step):
        return me + ((y_at + step) % Y_SIZE - y_at) * QUAD

    barrier = pltpu.get_barrier_semaphore()

    def greet(device):
        pl.semaphore_signal(barrier, inc=1, device_id=(device,), device_id_type=MESH)

    for peer in peers:
        greet(peer)

    loads = [
        pltpu.make_async_copy(src, dst, load_sem.at[i])
        for i, (src, dst) in enumerate(
            (
                (sends_hbm, sends_ref),
                (x_hbm, x_ref),
                (nb_hbm, nb_ref),
                (lw_hbm, lw_ref),
                (ct_hbm, ct_ref),
                (w_hbm, w_ref),
            )
        )
    ]
    for load in loads:
        load.start()

    for ring, size in ((along_z, Z_SIZE), (along_y, Y_SIZE)):
        greet(ring(1))
        greet(ring(size - 1))

    @pl.loop(1, PLACES)
    def _(step):
        greet(in_block(step))

    spreads = ((along_z, 1, Z_SIZE), (along_z, 2, Z_SIZE), (along_y, 1, Y_SIZE), (along_y, 1, Y_SIZE))

    def spread(k):
        ring, reach, size = spreads[k]
        for other in (reach, size - reach):
            pl.semaphore_signal(
                known.at[k], inc=1, device_id=(ring(other),), device_id_type=MESH
            )

    def heard(k):
        pl.semaphore_wait(known.at[k], 2)

    lane_low = lax.broadcasted_iota(jnp.int32, (CH // 2, 128), 1) < HALO

    def halo_copy(chain, step, place):
        return pltpu.make_async_remote_copy(
            src_ref=outgoing.at[chain, step, place],
            dst_ref=incoming.at[chain, step, place],
            send_sem=halo_send.at[chain, step],
            recv_sem=halo_recv.at[chain, step],
            device_id=(peers[place if chain == 0 else place ^ 1],),
            device_id_type=MESH,
        )

    def halo_all(chain, step):
        return pltpu.make_async_remote_copy(
            src_ref=outgoing.at[chain, step],
            dst_ref=incoming.at[chain, step],
            send_sem=halo_send.at[chain, step],
            recv_sem=halo_recv.at[chain, step],
            device_id=(peers[0],),
            device_id_type=MESH,
        )

    def post(chain, step, columns, start=True):
        for pair in range(PEERS // 2):
            block = columns[:, 128 * pair : 128 * pair + 128]
            upper, lower = block[: CH // 2], block[CH // 2 :]
            outgoing[chain, step, 2 * pair] = jnp.where(lane_low, upper, turned(lower))
            outgoing[chain, step, 2 * pair + 1] = jnp.where(lane_low, turned(upper), lower)
            if start:
                halo_copy(chain, step, 2 * pair).start()
                halo_copy(chain, step, 2 * pair + 1).start()

    def collect(chain, step):
        halo_all(chain, step).wait_recv()
        blocks = []
        for pair in range(PEERS // 2):
            one, two = incoming[chain, step, 2 * pair], incoming[chain, step, 2 * pair + 1]
            blocks.append(
                jnp.concatenate(
                    [jnp.where(lane_low, one, turned(two)), jnp.where(lane_low, turned(one), two)],
                    axis=0,
                )
            )
        return jnp.concatenate(blocks, axis=1)

    loads[0].wait()
    pixel = lax.broadcasted_iota(jnp.int32, (PIX, 128), 0)
    for pair in range(PEERS // 2):
        listed = jnp.concatenate(
            [sends_ref[ORDER[2 * pair + i] : ORDER[2 * pair + i] + 1, :] for i in range(2)], axis=1
        )
        s_mat[:, 128 * pair : 128 * pair + 128] = jnp.where(pixel == listed, 1.0, 0.0).astype(BF16)
    loads[1].wait()
    xs = [x_ref[...].astype(F32)]
    post(0, 0, dot(x_ref[...], s_mat[...]), start=False)
    loads[2].wait()
    slot = lax.broadcasted_iota(jnp.int32, (HALO, PIX), 0) + PIX
    for place, o in enumerate(ORDER):
        hit = slot + HALO * o == nb_ref[o + 1 : o + 2, :]
        t_mat[HALO * place : HALO * place + HALO, :] = jnp.where(hit, 1.0, 0.0).astype(BF16)
    loads[3].wait()
    lists = jnp.concatenate([lw_ref[o + 1 : o + 2, :] for o in ORDER], axis=0)
    high, rest = split(lists)
    middle = (lists - high.astype(F32)).astype(BF16)
    low = (lists - high.astype(F32) - middle.astype(F32)).astype(BF16)
    found = dot_nt(jnp.concatenate([high, middle, low], axis=0), t_mat[...])
    found = found[:PEERS] + found[PEERS : 2 * PEERS] + found[2 * PEERS :]
    own = lax.broadcasted_iota(jnp.int32, (PEERS, LISTED), 1) // HALO
    own = own == lax.broadcasted_iota(jnp.int32, (PEERS, LISTED), 0)
    list_weight = jnp.sum(jnp.where(own, found, 0.0), axis=0, keepdims=True)
    loads[4].wait()
    cs = [ct_ref[...].astype(F32)]
    post(1, 0, dot_nt(ct_ref[...], t_mat[...]) * list_weight, start=False)
    pl.semaphore_wait(barrier, PEERS + 4 + PLACES - 1)
    for chain in range(2):
        for place in range(PEERS):
            halo_copy(chain, 0, place).start()
    spread(0)

    for base in range(0, PIX, 32):
        column = lax.broadcasted_iota(jnp.int32, (32, PIX), 0) + base
        block = jnp.zeros((32, PIX), F32)
        for entry in range(STENCIL):
            block = block + jnp.where(
                column == nb_ref[entry : entry + 1, :], lw_ref[entry : entry + 1, :], 0.0
            )
        high, low = split(block)
        a_high[base : base + 32, :] = high
        a_low[base : base + 32, :] = low
    loads[5].wait()

    def near(value, times):
        return product(value, a_high[...], times) + times(value.astype(BF16), a_low[...])

    def out_term(k):
        return dot_tn(w_ref[CH * k : CH * k + CH, :], xs[k].astype(BF16))

    def mg_term(k):
        high, low = split(cs[k])
        weight = w_ref[CH * k : CH * k + CH, :]
        return dot(weight, high) + dot(weight, low)

    def inner(x, c):
        x_high, x_low = split(x)
        c_high, c_low = split(c)
        both = dot_nt(jnp.concatenate([x_high, x_low], axis=0), c_high)
        return both[:CH] + both[CH:] + dot_nt(x_high, c_low)

    class Batch:
        def __init__(self, which):
            self.which = which
            self.sums, self.block_in, self.part, self.place_in, self.total = sum_refs[
                5 * which : 5 * which + 5
            ]

        def copy(self, stage, src, dst, device):
            return pltpu.make_async_remote_copy(
                src_ref=src,
                dst_ref=dst,
                send_sem=sum_send.at[self.which, stage],
                recv_sem=sum_recv.at[self.which, stage],
                device_id=(device,),
                device_id_type=MESH,
            )

        def all_of(self, stage):
            ref = (self.block_in, self.place_in, self.total)[stage]
            ref = ref.at[pl.ds(0, (PLACES, blocks, PLACES)[stage] - 1)]
            return self.copy(stage, ref, ref, peers[0])

        def start(self, blocks):
            at = 0
            for block in blocks:
                n = block.shape[0] // PLACES
                for i in range(PLACES):
                    self.sums[i, at : at + n, :] = block[n * i : n * i + n]
                at += n

            @pl.loop(1, PLACES)
            def _(i):
                mine = self.sums.at[(my_place + i) % PLACES]
                self.copy(0, mine, self.block_in.at[my_place], in_block(i)).start()

            self.block_in[my_place] = self.sums[my_place]

        def across(self):
            self.all_of(0).wait_recv()
            piece = self.block_in[0]
            for i in range(1, PLACES):
                piece = piece + self.block_in[i]
            self.part[...] = piece

            @pl.loop(1, blocks)
            def _(i):
                self.copy(1, self.part, self.place_in.at[my_block], in_place(i)).start()

            self.place_in[my_block] = piece

        def back(self):
            self.all_of(1).wait_recv()
            piece = self.place_in[0]
            for i in range(1, blocks):
                piece = piece + self.place_in[i]
            self.total[my_place] = piece

            @pl.loop(1, PLACES)
            def _(i):
                mine = self.total.at[my_place]
                self.copy(2, mine, mine, in_block(i)).start()

        def arrive(self):
            self.all_of(2).wait_recv()

        def end(self):
            for stage in range(3):
                self.all_of(stage).wait_send()

    early, late = Batch(0), Batch(1)
    scale = 1.0 / math.sqrt(count * PIX)

    def halves(value):
        return jnp.concatenate([value[: CH // 2], value[CH // 2 :]], axis=1)

    out_sum = mg_sum = None
    for step in range(STEPS):
        x_near = near(xs[step], dot)
        c_near = near(cs[step], dot_nt)
        if step == 2:
            late.across()
        if step == 3:
            early.back()
            late.back()
        if step == 0:
            heard(0)
            spread(1)
            heard(1)
            spread(2)
        x_next = x_near + product(collect(0, step) * list_weight, t_mat[...], dot)
        if step:
            x_next = 2.0 * x_next - xs[step - 1]
        xs.append(x_next)
        if step + 1 < STEPS:
            listed = product(x_next, s_mat[...], dot)
        if step in (0, 2):
            post(0, step + 1, listed)
        if step == 1:
            none = jnp.zeros((CH, PIX), F32)
            last = inner(x_next, jnp.concatenate([cs[1], none], axis=0)) - half_early
        c_next = c_near + product(collect(1, step), s_mat[...], dot_nt)
        if step:
            c_next = 2.0 * c_next - cs[step - 1]
        cs.append(c_next)
        if step == 1:
            last = last + inner(x_next, jnp.concatenate([none, c_next], axis=0))
            late.start([last * (2.0 * scale)])
            post(0, step + 1, listed)
        if step + 1 < STEPS:
            post(1, step + 1, product(c_next, t_mat[...], dot_nt) * list_weight)
        if step == 0:
            p0 = dot_nt(x_ref[...], ct_ref[...])
            p1 = dot_nt(xs[1].astype(BF16), ct_ref[...])
            p2 = 2.0 * inner(xs[1], cs[1]) - p0
            half_early = 0.5 * jnp.concatenate([p1, p0], axis=1)
            early.start([scale * jnp.concatenate([p0, p1], axis=1), scale * halves(p2)])
            heard(2)
            spread(3)
        if step == 1:
            heard(3)
            early.across()
        if step < STEPS - 1:
            term_out, term_mg = out_term(step), mg_term(step)
            out_sum = term_out if out_sum is None else out_sum + term_out
            mg_sum = term_mg if mg_sum is None else mg_sum + term_mg

    for k in (STEPS - 1, STEPS):
        out_sum = out_sum + out_term(k)
        mg_sum = mg_sum + mg_term(k)
    out_ref[...] = out_sum.astype(BF16)
    mg_ref[...] = mg_sum.astype(BF16)
    early.arrive()

    def rows_of(batch, lower, upper):
        return jnp.concatenate([batch.total[i, lower:upper, :] for i in range(PLACES)], axis=0)

    first = rows_of(early, 0, 4)
    third = rows_of(early, 4, 6)
    wg_ref[0] = first[:, :CH]
    wg_ref[1] = first[:, CH:]
    wg_ref[2, : CH // 2] = third[:, :CH]
    wg_ref[2, CH // 2 :] = third[:, CH:]
    for chain in range(2):
        for step in range(STEPS):
            halo_all(chain, step).wait_send()
    early.end()
    late.arrive()
    second = rows_of(late, 0, 4)
    wg_ref[3] = second[:, :CH]
    wg_ref[4] = second[:, CH:]
    late.end()


def store_results(out_ref, mg_ref, wg_ref, out_hbm, mg_hbm, wg_hbm, sem):
    copies = [
        pltpu.make_async_copy(src, dst, sem.at[i])
        for i, (src, dst) in enumerate(((wg_ref, wg_hbm), (out_ref, out_hbm), (mg_ref, mg_hbm)))
    ]
    for copy in copies:
        copy.start()
    for copy in copies:
        copy.wait()


def solution(mesh):
    count = mesh.shape["pix"]
    blocks = count // PLACES
    dma = pltpu.SemaphoreType.DMA

    def local(input_maps, cheb_weights, cotangent, neighbours, lap_weights, send_rows):
        def body(*refs):
            kernel(count, *refs)

        results = pl.pallas_call(
            body,
            out_shape=(
                pltpu.VMEM((CH, PIX), BF16),
                pltpu.VMEM((CH, PIX), BF16),
                pltpu.VMEM((KTERMS, CH, CH), F32),
            ),
            in_specs=[pl.BlockSpec(memory_space=pltpu.HBM)] * 6,
            out_specs=tuple([pl.BlockSpec(memory_space=pltpu.VMEM)] * 3),
            scratch_shapes=[
                pltpu.VMEM((CH, PIX), BF16),
                pltpu.VMEM((KTERMS * CH, CH), BF16),
                pltpu.VMEM((CH, PIX), BF16),
                pltpu.VMEM((STENCIL, PIX), jnp.int32),
                pltpu.VMEM((STENCIL, PIX), F32),
                pltpu.VMEM((PEERS, HALO), jnp.int32),
                dma((6,)),
                pltpu.SemaphoreType.REGULAR((4,)),
                pltpu.VMEM((PIX, PIX), BF16),
                pltpu.VMEM((PIX, PIX), BF16),
                pltpu.VMEM((PIX, LISTED), BF16),
                pltpu.VMEM((LISTED, PIX), BF16),
                pltpu.VMEM((2, STEPS, PEERS, CH // 2, 128), F32),
                pltpu.VMEM((2, STEPS, PEERS, CH // 2, 128), F32),
                dma((2, STEPS)),
                dma((2, STEPS)),
                dma((2, 3)),
                dma((2, 3)),
                *[
                    pltpu.VMEM(lead + (share, 128), F32)
                    for share in SHARES
                    for lead in ((PLACES,), (PLACES,), (), (blocks,), (PLACES,))
                ],
            ],
            compiler_params=pltpu.CompilerParams(
                collective_id=0, has_side_effects=True, vmem_limit_bytes=16 * 1024 * 1024
            ),
        )(
            *[
                pltpu.with_memory_space_constraint(operand, pltpu.HBM)
                for operand in (
                    input_maps,
                    cheb_weights.reshape(KTERMS * CH, CH),
                    cotangent,
                    neighbours,
                    lap_weights,
                    send_rows,
                )
            ]
        )
        return pl.pallas_call(
            store_results,
            out_shape=tuple(jax.ShapeDtypeStruct(r.shape, r.dtype) for r in results),
            in_specs=[pl.BlockSpec(memory_space=pltpu.VMEM)] * 3,
            out_specs=tuple([pl.BlockSpec(memory_space=pltpu.HBM)] * 3),
            scratch_shapes=[dma((3,))],
        )(*[pltpu.with_memory_space_constraint(r, pltpu.VMEM) for r in results])

    return jax.shard_map(
        local,
        mesh=mesh,
        in_specs=(
            P(None, "pix"),
            P(),
            P(None, "pix"),
            P(None, "pix"),
            P(None, "pix"),
            P("pix", None),
        ),
        out_specs=(P(None, "pix"), P(None, "pix"), P()),
        check_vma=False,
    )
```

```python
import math

import jax
import jax.numpy as jnp
from jax import lax
from jax.experimental import pallas as pl
from jax.experimental.pallas import tpu as pltpu
from jax.sharding import PartitionSpec as P

CH = 64
KTERMS = 5
PIX = 256
HALO = 64
ROW = 16
QUAD, Y_SIZE, Z_SIZE, PLANE = 4, 4, 8, 128
PLACES = 16
PEERS = 8
STENCIL = 9
STEPS = KTERMS - 1
OFFSETS = [1, -1, 16, -16, 17, 15, -15, -17]
ORDER = [0, 1, 2, 3, 4, 7, 5, 6]
LISTED = PEERS * HALO
SHARES = [6, 4]
MESH = pl.DeviceIdType.MESH
F32 = jnp.float32
BF16 = jnp.bfloat16


def split(value):
    high = value.astype(BF16)
    return high, (value - high.astype(F32)).astype(BF16)


def dot(a, b):
    return jnp.dot(a, b, preferred_element_type=F32)


def dot_nt(a, b):
    return lax.dot_general(a, b, (((1,), (1,)), ((), ())), preferred_element_type=F32)


def dot_tn(a, b):
    return lax.dot_general(a, b, (((0,), (0,)), ((), ())), preferred_element_type=F32)


def product(value, matrix, times):
    high, low = split(value)
    both = times(jnp.concatenate([high, low], axis=0), matrix)
    rows = value.shape[0]
    return both[:rows] + both[rows:]


def turned(value):
    return pltpu.roll(value, HALO, 1)


def kernel(
    count,
    x_hbm,
    w_hbm,
    ct_hbm,
    nb_hbm,
    lw_hbm,
    sends_hbm,
    out_ref,
    mg_ref,
    wg_ref,
    x_ref,
    w_ref,
    ct_ref,
    nb_ref,
    lw_ref,
    sends_ref,
    load_sem,
    known,
    a_high,
    a_low,
    s_mat,
    t_mat,
    outgoing,
    incoming,
    halo_send,
    halo_recv,
    sum_send,
    sum_recv,
    *sum_refs,
):
    me = lax.axis_index("pix")
    blocks = count // PLACES
    x_at, z_at, y_at, quad_at = me // PLANE, me // ROW % Z_SIZE, me // QUAD % Y_SIZE, me % QUAD
    my_place, my_block = x_at * QUAD + quad_at, z_at * Y_SIZE + y_at
    peers = [(me + OFFSETS[o] + count) % count for o in ORDER]

    def device_at(place, block):
        return place // QUAD * PLANE + block // Y_SIZE * ROW + block % Y_SIZE * QUAD + place % QUAD

    def in_block(step):
        return device_at((my_place + step) % PLACES, my_block)

    def in_place(step):
        return device_at(my_place, (my_block + step) % blocks)

    def along_z(step):
        return me + ((z_at + step) % Z_SIZE - z_at) * ROW

    def along_y(step):
        return me + ((y_at + step) % Y_SIZE - y_at) * QUAD

    barrier = pltpu.get_barrier_semaphore()

    def greet(device):
        pl.semaphore_signal(barrier, inc=1, device_id=(device,), device_id_type=MESH)

    loads = [
        pltpu.make_async_copy(src, dst, load_sem.at[i])
        for i, (src, dst) in enumerate(
            (
                (sends_hbm, sends_ref),
                (x_hbm, x_ref),
                (nb_hbm, nb_ref),
                (lw_hbm, lw_ref),
                (ct_hbm, ct_ref),
                (w_hbm, w_ref),
            )
        )
    ]
    for load in loads:
        load.start()

    for peer in peers:
        greet(peer)

    for ring, size in ((along_z, Z_SIZE), (along_y, Y_SIZE)):
        greet(ring(1))
        greet(ring(size - 1))

    @pl.loop(1, PLACES)
    def _(step):
        greet(in_block(step))

    spreads = ((along_z, 1, Z_SIZE), (along_z, 2, Z_SIZE), (along_y, 1, Y_SIZE), (along_y, 1, Y_SIZE))

    def spread(k):
        ring, reach, size = spreads[k]
        for other in (reach, size - reach):
            pl.semaphore_signal(
                known.at[k], inc=1, device_id=(ring(other),), device_id_type=MESH
            )

    def heard(k):
        pl.semaphore_wait(known.at[k], 2)

    lane_low = lax.broadcasted_iota(jnp.int32, (CH // 2, 128), 1) < HALO

    def halo_copy(chain, step, place):
        return pltpu.make_async_remote_copy(
            src_ref=outgoing.at[chain, step, place],
            dst_ref=incoming.at[chain, step, place],
            send_sem=halo_send.at[chain, step],
            recv_sem=halo_recv.at[chain, step],
            device_id=(peers[place if chain == 0 else place ^ 1],),
            device_id_type=MESH,
        )

    def halo_all(chain, step):
        return pltpu.make_async_remote_copy(
            src_ref=outgoing.at[chain, step],
            dst_ref=incoming.at[chain, step],
            send_sem=halo_send.at[chain, step],
            recv_sem=halo_recv.at[chain, step],
            device_id=(peers[0],),
            device_id_type=MESH,
        )

    def post(chain, step, columns, start=True):
        for pair in range(PEERS // 2):
            block = columns[:, 128 * pair : 128 * pair + 128]
            upper, lower = block[: CH // 2], block[CH // 2 :]
            outgoing[chain, step, 2 * pair] = jnp.where(lane_low, upper, turned(lower))
            outgoing[chain, step, 2 * pair + 1] = jnp.where(lane_low, turned(upper), lower)
            if start:
                halo_copy(chain, step, 2 * pair).start()
                halo_copy(chain, step, 2 * pair + 1).start()

    def collect(chain, step):
        halo_all(chain, step).wait_recv()
        blocks = []
        for pair in range(PEERS // 2):
            one, two = incoming[chain, step, 2 * pair], incoming[chain, step, 2 * pair + 1]
            blocks.append(
                jnp.concatenate(
                    [jnp.where(lane_low, one, turned(two)), jnp.where(lane_low, turned(one), two)],
                    axis=0,
                )
            )
        return jnp.concatenate(blocks, axis=1)

    loads[0].wait()
    pixel = lax.broadcasted_iota(jnp.int32, (PIX, 128), 0)
    for pair in range(PEERS // 2):
        listed = jnp.concatenate(
            [sends_ref[ORDER[2 * pair + i] : ORDER[2 * pair + i] + 1, :] for i in range(2)], axis=1
        )
        s_mat[:, 128 * pair : 128 * pair + 128] = jnp.where(pixel == listed, 1.0, 0.0).astype(BF16)
    loads[1].wait()
    xs = [x_ref[...].astype(F32)]
    post(0, 0, dot(x_ref[...], s_mat[...]), start=False)
    loads[2].wait()
    slot = lax.broadcasted_iota(jnp.int32, (HALO, PIX), 0) + PIX
    for place, o in enumerate(ORDER):
        hit = slot + HALO * o == nb_ref[o + 1 : o + 2, :]
        t_mat[HALO * place : HALO * place + HALO, :] = jnp.where(hit, 1.0, 0.0).astype(BF16)
    loads[3].wait()
    lists = jnp.concatenate([lw_ref[o + 1 : o + 2, :] for o in ORDER], axis=0)
    high, rest = split(lists)
    middle = (lists - high.astype(F32)).astype(BF16)
    low = (lists - high.astype(F32) - middle.astype(F32)).astype(BF16)
    found = dot_nt(jnp.concatenate([high, middle, low], axis=0), t_mat[...])
    found = found[:PEERS] + found[PEERS : 2 * PEERS] + found[2 * PEERS :]
    own = lax.broadcasted_iota(jnp.int32, (PEERS, LISTED), 1) // HALO
    own = own == lax.broadcasted_iota(jnp.int32, (PEERS, LISTED), 0)
    list_weight = jnp.sum(jnp.where(own, found, 0.0), axis=0, keepdims=True)
    loads[4].wait()
    cs = [ct_ref[...].astype(F32)]
    post(1, 0, dot_nt(ct_ref[...], t_mat[...]) * list_weight, start=False)
    pl.semaphore_wait(barrier, PEERS + 4 + PLACES - 1)
    for chain in range(2):
        for place in range(PEERS):
            halo_copy(chain, 0, place).start()
    spread(0)

    for base in range(0, PIX, 32):
        column = lax.broadcasted_iota(jnp.int32, (32, PIX), 0) + base
        block = jnp.zeros((32, PIX), F32)
        for entry in range(STENCIL):
            block = block + jnp.where(
                column == nb_ref[entry : entry + 1, :], lw_ref[entry : entry + 1, :], 0.0
            )
        high, low = split(block)
        a_high[base : base + 32, :] = high
        a_low[base : base + 32, :] = low
    loads[5].wait()

    def near(value, times):
        return product(value, a_high[...], times) + times(value.astype(BF16), a_low[...])

    def out_term(k):
        return dot_tn(w_ref[CH * k : CH * k + CH, :], xs[k].astype(BF16))

    def mg_term(k):
        high, low = split(cs[k])
        weight = w_ref[CH * k : CH * k + CH, :]
        return dot(weight, high) + dot(weight, low)

    def inner(x, c):
        x_high, x_low = split(x)
        c_high, c_low = split(c)
        both = dot_nt(jnp.concatenate([x_high, x_low], axis=0), c_high)
        return both[:CH] + both[CH:] + dot_nt(x_high, c_low)

    class Batch:
        def __init__(self, which):
            self.which = which
            self.sums, self.block_in, self.part, self.place_in, self.total = sum_refs[
                5 * which : 5 * which + 5
            ]

        def copy(self, stage, src, dst, device):
            return pltpu.make_async_remote_copy(
                src_ref=src,
                dst_ref=dst,
                send_sem=sum_send.at[self.which, stage],
                recv_sem=sum_recv.at[self.which, stage],
                device_id=(device,),
                device_id_type=MESH,
            )

        def all_of(self, stage):
            ref = (self.block_in, self.place_in, self.total)[stage]
            ref = ref.at[pl.ds(0, (PLACES, blocks, PLACES)[stage] - 1)]
            return self.copy(stage, ref, ref, peers[0])

        def start(self, blocks):
            at = 0
            for block in blocks:
                n = block.shape[0] // PLACES
                for i in range(PLACES):
                    self.sums[i, at : at + n, :] = block[n * i : n * i + n]
                at += n

            for i in range(1, PLACES):
                mine = self.sums.at[(my_place + i) % PLACES]
                self.copy(0, mine, self.block_in.at[my_place], in_block(i)).start()

            self.block_in[my_place] = self.sums[my_place]

        def across(self):
            self.all_of(0).wait_recv()
            piece = self.block_in[0]
            for i in range(1, PLACES):
                piece = piece + self.block_in[i]
            self.part[...] = piece

            for i in range(1, blocks):
                self.copy(1, self.part, self.place_in.at[my_block], in_place(i)).start()

            self.place_in[my_block] = piece

        def back(self):
            self.all_of(1).wait_recv()
            piece = self.place_in[0]
            for i in range(1, blocks):
                piece = piece + self.place_in[i]
            self.total[my_place] = piece

            for i in range(1, PLACES):
                mine = self.total.at[my_place]
                self.copy(2, mine, mine, in_block(i)).start()

        def arrive(self):
            self.all_of(2).wait_recv()

        def end(self):
            for stage in range(3):
                self.all_of(stage).wait_send()

    early, late = Batch(0), Batch(1)
    scale = 1.0 / math.sqrt(count * PIX)

    def halves(value):
        return jnp.concatenate([value[: CH // 2], value[CH // 2 :]], axis=1)

    out_sum = mg_sum = None
    for step in range(STEPS):
        x_near = near(xs[step], dot)
        c_near = near(cs[step], dot_nt)
        if step == 2:
            late.across()
        if step == 3:
            early.back()
            late.back()
        if step == 0:
            heard(0)
            spread(1)
            heard(1)
            spread(2)
        x_next = x_near + product(collect(0, step) * list_weight, t_mat[...], dot)
        if step:
            x_next = 2.0 * x_next - xs[step - 1]
        xs.append(x_next)
        if step + 1 < STEPS:
            listed = product(x_next, s_mat[...], dot)
        if step in (0, 2):
            post(0, step + 1, listed)
        if step == 1:
            none = jnp.zeros((CH, PIX), F32)
            last = inner(x_next, jnp.concatenate([cs[1], none], axis=0)) - half_early
        c_next = c_near + product(collect(1, step), s_mat[...], dot_nt)
        if step:
            c_next = 2.0 * c_next - cs[step - 1]
        cs.append(c_next)
        if step == 1:
            last = last + inner(x_next, jnp.concatenate([none, c_next], axis=0))
            late.start([last * (2.0 * scale)])
            post(0, step + 1, listed)
        if step + 1 < STEPS:
            post(1, step + 1, product(c_next, t_mat[...], dot_nt) * list_weight)
        if step == 0:
            p0 = dot_nt(x_ref[...], ct_ref[...])
            p1 = dot_nt(xs[1].astype(BF16), ct_ref[...])
            p2 = 2.0 * inner(xs[1], cs[1]) - p0
            half_early = 0.5 * jnp.concatenate([p1, p0], axis=1)
            early.start([scale * jnp.concatenate([p0, p1], axis=1), scale * halves(p2)])
            heard(2)
            spread(3)
        if step == 1:
            heard(3)
            early.across()
        if step < STEPS - 1:
            term_out, term_mg = out_term(step), mg_term(step)
            out_sum = term_out if out_sum is None else out_sum + term_out
            mg_sum = term_mg if mg_sum is None else mg_sum + term_mg

    for k in (STEPS - 1, STEPS):
        out_sum = out_sum + out_term(k)
        mg_sum = mg_sum + mg_term(k)
    out_ref[...] = out_sum.astype(BF16)
    mg_ref[...] = mg_sum.astype(BF16)
    early.arrive()

    def rows_of(batch, lower, upper):
        return jnp.concatenate([batch.total[i, lower:upper, :] for i in range(PLACES)], axis=0)

    first = rows_of(early, 0, 4)
    third = rows_of(early, 4, 6)
    wg_ref[0] = first[:, :CH]
    wg_ref[1] = first[:, CH:]
    wg_ref[2, : CH // 2] = third[:, :CH]
    wg_ref[2, CH // 2 :] = third[:, CH:]
    for chain in range(2):
        for step in range(STEPS):
            halo_all(chain, step).wait_send()
    early.end()
    late.arrive()
    second = rows_of(late, 0, 4)
    wg_ref[3] = second[:, :CH]
    wg_ref[4] = second[:, CH:]
    late.end()


def store_results(out_ref, mg_ref, wg_ref, out_hbm, mg_hbm, wg_hbm, sem):
    copies = [
        pltpu.make_async_copy(src, dst, sem.at[i])
        for i, (src, dst) in enumerate(((wg_ref, wg_hbm), (out_ref, out_hbm), (mg_ref, mg_hbm)))
    ]
    for copy in copies:
        copy.start()
    for copy in copies:
        copy.wait()


def solution(mesh):
    count = mesh.shape["pix"]
    blocks = count // PLACES
    dma = pltpu.SemaphoreType.DMA

    def local(input_maps, cheb_weights, cotangent, neighbours, lap_weights, send_rows):
        def body(*refs):
            kernel(count, *refs)

        results = pl.pallas_call(
            body,
            out_shape=(
                pltpu.VMEM((CH, PIX), BF16),
                pltpu.VMEM((CH, PIX), BF16),
                pltpu.VMEM((KTERMS, CH, CH), F32),
            ),
            in_specs=[pl.BlockSpec(memory_space=pltpu.HBM)] * 6,
            out_specs=tuple([pl.BlockSpec(memory_space=pltpu.VMEM)] * 3),
            scratch_shapes=[
                pltpu.VMEM((CH, PIX), BF16),
                pltpu.VMEM((KTERMS * CH, CH), BF16),
                pltpu.VMEM((CH, PIX), BF16),
                pltpu.VMEM((STENCIL, PIX), jnp.int32),
                pltpu.VMEM((STENCIL, PIX), F32),
                pltpu.VMEM((PEERS, HALO), jnp.int32),
                dma((6,)),
                pltpu.SemaphoreType.REGULAR((4,)),
                pltpu.VMEM((PIX, PIX), BF16),
                pltpu.VMEM((PIX, PIX), BF16),
                pltpu.VMEM((PIX, LISTED), BF16),
                pltpu.VMEM((LISTED, PIX), BF16),
                pltpu.VMEM((2, STEPS, PEERS, CH // 2, 128), F32),
                pltpu.VMEM((2, STEPS, PEERS, CH // 2, 128), F32),
                dma((2, STEPS)),
                dma((2, STEPS)),
                dma((2, 3)),
                dma((2, 3)),
                *[
                    pltpu.VMEM(lead + (share, 128), F32)
                    for share in SHARES
                    for lead in ((PLACES,), (PLACES,), (), (blocks,), (PLACES,))
                ],
            ],
            compiler_params=pltpu.CompilerParams(
                collective_id=0, has_side_effects=True, vmem_limit_bytes=16 * 1024 * 1024
            ),
        )(
            *[
                pltpu.with_memory_space_constraint(operand, pltpu.HBM)
                for operand in (
                    input_maps,
                    cheb_weights.reshape(KTERMS * CH, CH),
                    cotangent,
                    neighbours,
                    lap_weights,
                    send_rows,
                )
            ]
        )
        return pl.pallas_call(
            store_results,
            out_shape=tuple(jax.ShapeDtypeStruct(r.shape, r.dtype) for r in results),
            in_specs=[pl.BlockSpec(memory_space=pltpu.VMEM)] * 3,
            out_specs=tuple([pl.BlockSpec(memory_space=pltpu.HBM)] * 3),
            scratch_shapes=[dma((3,))],
        )(*[pltpu.with_memory_space_constraint(r, pltpu.VMEM) for r in results])

    return jax.shard_map(
        local,
        mesh=mesh,
        in_specs=(
            P(None, "pix"),
            P(),
            P(None, "pix"),
            P(None, "pix"),
            P(None, "pix"),
            P("pix", None),
        ),
        out_specs=(P(None, "pix"), P(None, "pix"), P()),
        check_vma=False,
    )
```

```python
import math

import jax
import jax.numpy as jnp
from jax import lax
from jax.experimental import pallas as pl
from jax.experimental.pallas import tpu as pltpu
from jax.sharding import PartitionSpec as P

CH = 64
KTERMS = 5
PIX = 256
HALO = 64
ROW = 16
QUAD, Y_SIZE, Z_SIZE, PLANE = 4, 4, 8, 128
PLACES = 16
PEERS = 8
STENCIL = 9
STEPS = KTERMS - 1
OFFSETS = [1, -1, 16, -16, 17, 15, -15, -17]
ORDER = [0, 1, 2, 3, 4, 7, 5, 6]
LISTED = PEERS * HALO
SHARES = [6, 4]
MESH = pl.DeviceIdType.MESH
F32 = jnp.float32
BF16 = jnp.bfloat16


def split(value):
    high = value.astype(BF16)
    return high, (value - high.astype(F32)).astype(BF16)


def dot(a, b):
    return jnp.dot(a, b, preferred_element_type=F32)


def dot_nt(a, b):
    return lax.dot_general(a, b, (((1,), (1,)), ((), ())), preferred_element_type=F32)


def dot_tn(a, b):
    return lax.dot_general(a, b, (((0,), (0,)), ((), ())), preferred_element_type=F32)


def product(value, matrix, times):
    high, low = split(value)
    both = times(jnp.concatenate([high, low], axis=0), matrix)
    rows = value.shape[0]
    return both[:rows] + both[rows:]


def added(terms):
    while len(terms) > 1:
        half = len(terms) // 2
        terms = [a + b for a, b in zip(terms[:half], terms[half:])]
    return terms[0]


def turned(value):
    return pltpu.roll(value, HALO, 1)


def kernel(
    count,
    x_hbm,
    w_hbm,
    ct_hbm,
    nb_hbm,
    lw_hbm,
    sends_hbm,
    out_ref,
    mg_ref,
    wg_ref,
    x_ref,
    w_ref,
    ct_ref,
    nb_ref,
    lw_ref,
    sends_ref,
    load_sem,
    known,
    a_high,
    a_low,
    s_mat,
    t_mat,
    outgoing,
    incoming,
    halo_send,
    halo_recv,
    sum_send,
    sum_recv,
    *sum_refs,
):
    me = lax.axis_index("pix")
    blocks = count // PLACES
    x_at, z_at, y_at, quad_at = me // PLANE, me // ROW % Z_SIZE, me // QUAD % Y_SIZE, me % QUAD
    my_place, my_block = x_at * QUAD + quad_at, z_at * Y_SIZE + y_at
    peers = [(me + OFFSETS[o] + count) % count for o in ORDER]

    def device_at(place, block):
        return place // QUAD * PLANE + block // Y_SIZE * ROW + block % Y_SIZE * QUAD + place % QUAD

    def in_block(step):
        return device_at((my_place + step) % PLACES, my_block)

    def in_place(step):
        return device_at(my_place, (my_block + step) % blocks)

    def along_z(step):
        return me + ((z_at + step) % Z_SIZE - z_at) * ROW

    def along_y(step):
        return me + ((y_at + step) % Y_SIZE - y_at) * QUAD

    barrier = pltpu.get_barrier_semaphore()

    def greet(device):
        pl.semaphore_signal(barrier, inc=1, device_id=(device,), device_id_type=MESH)

    loads = [
        pltpu.make_async_copy(src, dst, load_sem.at[i])
        for i, (src, dst) in enumerate(
            (
                (sends_hbm, sends_ref),
                (x_hbm, x_ref),
                (nb_hbm, nb_ref),
                (lw_hbm, lw_ref),
                (ct_hbm, ct_ref),
                (w_hbm, w_ref),
            )
        )
    ]
    for load in loads:
        load.start()

    for peer in peers:
        greet(peer)

    for ring, size in ((along_z, Z_SIZE), (along_y, Y_SIZE)):
        greet(ring(1))
        greet(ring(size - 1))

    others = [((my_place + i) % PLACES, in_block(i)) for i in range(1, PLACES)]
    for _, device in others:
        greet(device)

    spreads = ((along_z, 1, Z_SIZE), (along_z, 2, Z_SIZE), (along_y, 1, Y_SIZE), (along_y, 1, Y_SIZE))

    def spread(k):
        ring, reach, size = spreads[k]
        for other in (reach, size - reach):
            pl.semaphore_signal(
                known.at[k], inc=1, device_id=(ring(other),), device_id_type=MESH
            )

    def heard(k):
        pl.semaphore_wait(known.at[k], 2)

    lane_low = lax.broadcasted_iota(jnp.int32, (CH // 2, 128), 1) < HALO

    def halo_copy(chain, step, place):
        return pltpu.make_async_remote_copy(
            src_ref=outgoing.at[chain, step, place],
            dst_ref=incoming.at[chain, step, place],
            send_sem=halo_send.at[chain, step],
            recv_sem=halo_recv.at[chain, step],
            device_id=(peers[place if chain == 0 else place ^ 1],),
            device_id_type=MESH,
        )

    def halo_all(chain, step):
        return pltpu.make_async_remote_copy(
            src_ref=outgoing.at[chain, step],
            dst_ref=incoming.at[chain, step],
            send_sem=halo_send.at[chain, step],
            recv_sem=halo_recv.at[chain, step],
            device_id=(peers[0],),
            device_id_type=MESH,
        )

    def post(chain, step, columns, start=True):
        for pair in range(PEERS // 2):
            block = columns[:, 128 * pair : 128 * pair + 128]
            upper, lower = block[: CH // 2], block[CH // 2 :]
            outgoing[chain, step, 2 * pair] = jnp.where(lane_low, upper, turned(lower))
            outgoing[chain, step, 2 * pair + 1] = jnp.where(lane_low, turned(upper), lower)
            if start:
                halo_copy(chain, step, 2 * pair).start()
                halo_copy(chain, step, 2 * pair + 1).start()

    def collect(chain, step):
        halo_all(chain, step).wait_recv()
        blocks = []
        for pair in range(PEERS // 2):
            one, two = incoming[chain, step, 2 * pair], incoming[chain, step, 2 * pair + 1]
            blocks.append(
                jnp.concatenate(
                    [jnp.where(lane_low, one, turned(two)), jnp.where(lane_low, turned(one), two)],
                    axis=0,
                )
            )
        return jnp.concatenate(blocks, axis=1)

    loads[0].wait()
    pixel = lax.broadcasted_iota(jnp.int32, (PIX, 128), 0)
    for pair in range(PEERS // 2):
        listed = jnp.concatenate(
            [sends_ref[ORDER[2 * pair + i] : ORDER[2 * pair + i] + 1, :] for i in range(2)], axis=1
        )
        s_mat[:, 128 * pair : 128 * pair + 128] = jnp.where(pixel == listed, 1.0, 0.0).astype(BF16)
    loads[1].wait()
    xs = [x_ref[...].astype(F32)]
    post(0, 0, dot(x_ref[...], s_mat[...]), start=False)
    loads[2].wait()
    slot = lax.broadcasted_iota(jnp.int32, (HALO, PIX), 0) + PIX
    for place, o in enumerate(ORDER):
        hit = slot + HALO * o == nb_ref[o + 1 : o + 2, :]
        t_mat[HALO * place : HALO * place + HALO, :] = jnp.where(hit, 1.0, 0.0).astype(BF16)
    loads[3].wait()
    lists = jnp.concatenate([lw_ref[o + 1 : o + 2, :] for o in ORDER], axis=0)
    high, rest = split(lists)
    middle = (lists - high.astype(F32)).astype(BF16)
    low = (lists - high.astype(F32) - middle.astype(F32)).astype(BF16)
    found = dot_nt(jnp.concatenate([high, middle, low], axis=0), t_mat[...])
    found = found[:PEERS] + found[PEERS : 2 * PEERS] + found[2 * PEERS :]
    own = lax.broadcasted_iota(jnp.int32, (PEERS, LISTED), 1) // HALO
    own = own == lax.broadcasted_iota(jnp.int32, (PEERS, LISTED), 0)
    list_weight = jnp.sum(jnp.where(own, found, 0.0), axis=0, keepdims=True)
    loads[4].wait()
    cs = [ct_ref[...].astype(F32)]
    post(1, 0, dot_nt(ct_ref[...], t_mat[...]) * list_weight, start=False)
    pl.semaphore_wait(barrier, PEERS + 4 + PLACES - 1)
    for chain in range(2):
        for place in range(PEERS):
            halo_copy(chain, 0, place).start()
    like_placed = [in_place(i) for i in range(1, blocks)]
    spread(0)

    for base in range(0, PIX, 32):
        column = lax.broadcasted_iota(jnp.int32, (32, PIX), 0) + base
        block = jnp.zeros((32, PIX), F32)
        for entry in range(STENCIL):
            block = block + jnp.where(
                column == nb_ref[entry : entry + 1, :], lw_ref[entry : entry + 1, :], 0.0
            )
        high, low = split(block)
        a_high[base : base + 32, :] = high
        a_low[base : base + 32, :] = low
    loads[5].wait()

    def near(value, times):
        return product(value, a_high[...], times) + times(value.astype(BF16), a_low[...])

    def out_term(k):
        return dot_tn(w_ref[CH * k : CH * k + CH, :], xs[k].astype(BF16))

    def mg_term(k):
        high, low = split(cs[k])
        weight = w_ref[CH * k : CH * k + CH, :]
        return dot(weight, high) + dot(weight, low)

    def inner(x, c):
        x_high, x_low = split(x)
        c_high, c_low = split(c)
        both = dot_nt(jnp.concatenate([x_high, x_low], axis=0), c_high)
        return both[:CH] + both[CH:] + dot_nt(x_high, c_low)

    class Batch:
        def __init__(self, which):
            self.which = which
            self.sums, self.block_in, self.part, self.place_in, self.total = sum_refs[
                5 * which : 5 * which + 5
            ]

        def copy(self, stage, src, dst, device):
            return pltpu.make_async_remote_copy(
                src_ref=src,
                dst_ref=dst,
                send_sem=sum_send.at[self.which, stage],
                recv_sem=sum_recv.at[self.which, stage],
                device_id=(device,),
                device_id_type=MESH,
            )

        def all_of(self, stage):
            ref = (self.block_in, self.place_in, self.total)[stage]
            ref = ref.at[pl.ds(0, (PLACES, blocks, PLACES)[stage] - 1)]
            return self.copy(stage, ref, ref, peers[0])

        def start(self, blocks):
            at = 0
            for block in blocks:
                n = block.shape[0] // PLACES
                for i in range(PLACES):
                    self.sums[i, at : at + n, :] = block[n * i : n * i + n]
                at += n

            for place, device in others:
                mine = self.sums.at[place]
                self.copy(0, mine, self.block_in.at[my_place], device).start()

            self.block_in[my_place] = self.sums[my_place]

        def across(self):
            self.all_of(0).wait_recv()
            piece = added([self.block_in[i] for i in range(PLACES)])
            self.part[...] = piece

            for device in like_placed:
                self.copy(1, self.part, self.place_in.at[my_block], device).start()

            self.place_in[my_block] = piece

        def back(self):
            self.all_of(1).wait_recv()
            piece = added([self.place_in[i] for i in range(blocks)])
            self.total[my_place] = piece

            mine = self.total.at[my_place]
            for _, device in others:
                self.copy(2, mine, mine, device).start()

        def arrive(self):
            self.all_of(2).wait_recv()

        def end(self):
            for stage in range(3):
                self.all_of(stage).wait_send()

    early, late = Batch(0), Batch(1)
    scale = 1.0 / math.sqrt(count * PIX)

    def halves(value):
        return jnp.concatenate([value[: CH // 2], value[CH // 2 :]], axis=1)

    out_sum = mg_sum = None
    for step in range(STEPS):
        x_near = near(xs[step], dot)
        c_near = near(cs[step], dot_nt)
        if step == 2:
            late.across()
        if step == 3:
            early.back()
            late.back()
        if step == 0:
            heard(0)
            spread(1)
            heard(1)
            spread(2)
        x_next = x_near + product(collect(0, step) * list_weight, t_mat[...], dot)
        if step:
            x_next = 2.0 * x_next - xs[step - 1]
        xs.append(x_next)
        if step + 1 < STEPS:
            listed = product(x_next, s_mat[...], dot)
        if step in (0, 2):
            post(0, step + 1, listed)
        if step == 1:
            none = jnp.zeros((CH, PIX), F32)
            last = inner(x_next, jnp.concatenate([cs[1], none], axis=0)) - half_early
        c_next = c_near + product(collect(1, step), s_mat[...], dot_nt)
        if step:
            c_next = 2.0 * c_next - cs[step - 1]
        cs.append(c_next)
        if step == 1:
            last = last + inner(x_next, jnp.concatenate([none, c_next], axis=0))
            late.start([last * (2.0 * scale)])
            post(0, step + 1, listed)
        if step + 1 < STEPS:
            post(1, step + 1, product(c_next, t_mat[...], dot_nt) * list_weight)
        if step == 0:
            p0 = dot_nt(x_ref[...], ct_ref[...])
            p1 = dot_nt(xs[1].astype(BF16), ct_ref[...])
            p2 = 2.0 * inner(xs[1], cs[1]) - p0
            half_early = 0.5 * jnp.concatenate([p1, p0], axis=1)
            early.start([scale * jnp.concatenate([p0, p1], axis=1), scale * halves(p2)])
            heard(2)
            spread(3)
        if step == 1:
            heard(3)
            early.across()
        if step < STEPS - 1:
            term_out, term_mg = out_term(step), mg_term(step)
            out_sum = term_out if out_sum is None else out_sum + term_out
            mg_sum = term_mg if mg_sum is None else mg_sum + term_mg

    for k in (STEPS - 1, STEPS):
        out_sum = out_sum + out_term(k)
        mg_sum = mg_sum + mg_term(k)
    out_ref[...] = out_sum.astype(BF16)
    mg_ref[...] = mg_sum.astype(BF16)
    early.arrive()

    def rows_of(batch, lower, upper):
        return jnp.concatenate([batch.total[i, lower:upper, :] for i in range(PLACES)], axis=0)

    first = rows_of(early, 0, 4)
    third = rows_of(early, 4, 6)
    wg_ref[0] = first[:, :CH]
    wg_ref[1] = first[:, CH:]
    wg_ref[2, : CH // 2] = third[:, :CH]
    wg_ref[2, CH // 2 :] = third[:, CH:]
    for chain in range(2):
        for step in range(STEPS):
            halo_all(chain, step).wait_send()
    early.end()
    late.arrive()
    second = rows_of(late, 0, 4)
    wg_ref[3] = second[:, :CH]
    wg_ref[4] = second[:, CH:]
    late.end()


def store_results(out_ref, mg_ref, wg_ref, out_hbm, mg_hbm, wg_hbm, sem):
    copies = [
        pltpu.make_async_copy(src, dst, sem.at[i])
        for i, (src, dst) in enumerate(((wg_ref, wg_hbm), (out_ref, out_hbm), (mg_ref, mg_hbm)))
    ]
    for copy in copies:
        copy.start()
    for copy in copies:
        copy.wait()


def solution(mesh):
    count = mesh.shape["pix"]
    blocks = count // PLACES
    dma = pltpu.SemaphoreType.DMA

    def local(input_maps, cheb_weights, cotangent, neighbours, lap_weights, send_rows):
        def body(*refs):
            kernel(count, *refs)

        results = pl.pallas_call(
            body,
            out_shape=(
                pltpu.VMEM((CH, PIX), BF16),
                pltpu.VMEM((CH, PIX), BF16),
                pltpu.VMEM((KTERMS, CH, CH), F32),
            ),
            in_specs=[pl.BlockSpec(memory_space=pltpu.HBM)] * 6,
            out_specs=tuple([pl.BlockSpec(memory_space=pltpu.VMEM)] * 3),
            scratch_shapes=[
                pltpu.VMEM((CH, PIX), BF16),
                pltpu.VMEM((KTERMS * CH, CH), BF16),
                pltpu.VMEM((CH, PIX), BF16),
                pltpu.VMEM((STENCIL, PIX), jnp.int32),
                pltpu.VMEM((STENCIL, PIX), F32),
                pltpu.VMEM((PEERS, HALO), jnp.int32),
                dma((6,)),
                pltpu.SemaphoreType.REGULAR((4,)),
                pltpu.VMEM((PIX, PIX), BF16),
                pltpu.VMEM((PIX, PIX), BF16),
                pltpu.VMEM((PIX, LISTED), BF16),
                pltpu.VMEM((LISTED, PIX), BF16),
                pltpu.VMEM((2, STEPS, PEERS, CH // 2, 128), F32),
                pltpu.VMEM((2, STEPS, PEERS, CH // 2, 128), F32),
                dma((2, STEPS)),
                dma((2, STEPS)),
                dma((2, 3)),
                dma((2, 3)),
                *[
                    pltpu.VMEM(lead + (share, 128), F32)
                    for share in SHARES
                    for lead in ((PLACES,), (PLACES,), (), (blocks,), (PLACES,))
                ],
            ],
            compiler_params=pltpu.CompilerParams(
                collective_id=0, has_side_effects=True, vmem_limit_bytes=16 * 1024 * 1024
            ),
        )(
            *[
                pltpu.with_memory_space_constraint(operand, pltpu.HBM)
                for operand in (
                    input_maps,
                    cheb_weights.reshape(KTERMS * CH, CH),
                    cotangent,
                    neighbours,
                    lap_weights,
                    send_rows,
                )
            ]
        )
        return pl.pallas_call(
            store_results,
            out_shape=tuple(jax.ShapeDtypeStruct(r.shape, r.dtype) for r in results),
            in_specs=[pl.BlockSpec(memory_space=pltpu.VMEM)] * 3,
            out_specs=tuple([pl.BlockSpec(memory_space=pltpu.HBM)] * 3),
            scratch_shapes=[dma((3,))],
        )(*[pltpu.with_memory_space_constraint(r, pltpu.VMEM) for r in results])

    return jax.shard_map(
        local,
        mesh=mesh,
        in_specs=(
            P(None, "pix"),
            P(),
            P(None, "pix"),
            P(None, "pix"),
            P(None, "pix"),
            P("pix", None),
        ),
        out_specs=(P(None, "pix"), P(None, "pix"), P()),
        check_vma=False,
    )
```
